32 devices in a mesh: group: 4 (over x, core), seq: 2 (over y), tp: 4 (over z).
Axes of the slice: x: 2, y: 2, z: 4, core: 2. Of those that a mesh axis runs over, the one named last changes fastest.
Arguments:
- hidden: bfloat16 [2048, 5120], P(('group', 'seq')), may hold values from -6 to 6
- norm_gain: bfloat16 [5120], replicated, may hold values from 0.5 to 1.5
- gen_value: bfloat16 [5120, 2560], P('seq', 'tp'), may hold values from -0.078125 to 0.078125
- gen_head: bfloat16 [2560, 64], P('tp'), may hold values from -0.125 to 0.125
- critic_embed: bfloat16 [2, 64, 5120], replicated, may hold values from -0.75 to 0.75
- critic_gain: bfloat16 [2, 5120], replicated, may hold values from 0.5 to 1.5
- critic_value: bfloat16 [5120, 5120], P('seq', ('group', 'tp')), may hold values from -0.078125 to 0.078125
- critic_head: bfloat16 [5120, 64], P(('group', 'tp')), may hold values from -0.125 to 0.125
- noise: bfloat16 [2048, 64], P('seq'), may hold values from -6 to 6
- owner: int32 [2048], P(('group', 'seq')), may hold values from 0 to 2047, as said below
- tsteps: int32 [1], replicated, may hold values from 0 to 999
- noise_mix: float32 [2, 1000], replicated, may hold values from 0.3 to 1
- gap_weight: float32 [1000], replicated, may hold values from 2 to 16
Outputs:
- gen_latent: bfloat16 [2048, 64], P(('group', 'seq'))
- grad_hidden: bfloat16 [2048, 5120], P(('group', 'seq'), 'tp')
The draws below stay inside these ranges and needn't reach their ends.
Inputs may be any that keep to these rules, and one draw needn't show every extreme that they name: owner is a permutation of the token positions. The 256 tokens of one generator block (aligned blocks of 256) place at most 255 tokens in one critic position block (aligned blocks of 1024 positions), and exactly 255 in some; every critic position block receives tokens from every generator block.
All inputs are finite; a program needn't handle non-finite values.
Results may differ from the reference program's by a relative error of at most 0.035.
Values may be sent and summed in bfloat16 or wider, within the bound.
A program may use at most 128 MiB of HBM per device.

```python
import math
import jax
import jax.numpy as jnp
from jax import lax

D = 5120
HW = 2560
C = 64
R = 256
FTOK = 2048
NT = 1000
TOKENS = 2048
FRAMES = 1
CRIT_ROWS = 1024
N_TP = 4


def draw_owner(key, part):
    key = jax.random.fold_in(key, 11)
    shards = TOKENS // R
    seq_count = TOKENS // CRIT_ROWS
    pair = R // seq_count
    spread = pair - 1
    key_src, key_dst, key_place, key_order = jax.random.split(key, 4)
    src_sign = jnp.where(jax.random.permutation(key_src, shards) < shards // 2, 1, -1)
    dst_sign = jnp.where(jax.random.permutation(key_dst, seq_count) < seq_count // 2, 1, -1)
    counts = pair + spread * src_sign[:, None] * dst_sign[None, :]
    inclusive = jnp.cumsum(counts, axis=1)
    exclusive = inclusive - counts
    below = jnp.cumsum(counts, axis=0) - counts
    ranks = jnp.arange(R)
    target = jnp.sum((inclusive[:, None, :] <= ranks[None, :, None]).astype(jnp.int32), axis=2)
    offset = jnp.take_along_axis(below, target, axis=1) + ranks[None, :] - jnp.take_along_axis(exclusive, target, axis=1)
    shuffles = jax.vmap(lambda k: jax.random.permutation(k, CRIT_ROWS))(jax.random.split(key_place, seq_count))
    position = target * CRIT_ROWS + shuffles[target, offset]
    orders = jax.vmap(lambda k: jax.random.permutation(k, R))(jax.random.split(key_order, shards))
    flat_index = (jnp.arange(shards)[:, None] * R + orders).reshape(-1)
    return jnp.zeros((TOKENS,), jnp.int32).at[flat_index].set(position.reshape(-1).astype(jnp.int32))


def block_scale(own_key, dims, cuts, low, largest):
    level = 1.0
    for dim, shards_of in cuts:
        heights = jax.random.uniform(jax.random.fold_in(jax.random.fold_in(own_key, 6), dim), (shards_of,), jnp.float32, low / len(cuts), largest / len(cuts))
        level = level * jnp.repeat(jnp.exp(heights), dims[dim] // shards_of).reshape((-1,) + (1,) * (len(dims) - 1 - dim))
    return level


def scatter_about(rng, shape, width, bound, cuts=(), kind=jnp.bfloat16):
    values = width * jax.random.normal(rng, shape, jnp.float32)
    if cuts:
        values = values * block_scale(rng, shape, cuts, -0.22, 0.18)
    return jnp.clip(values, -bound, bound).astype(kind)


def setup_inputs(seed: int = 0) -> dict:
    seeds = jax.random.split(jax.random.key(seed), 14)
    hidden = scatter_about(seeds[0], (TOKENS, D), 1.0, 6.0, ((0, 8),))
    norm_gain = jnp.clip(1.0 + 0.1 * jax.random.normal(seeds[1], (D,), jnp.float32), 0.5, 1.5).astype(jnp.bfloat16)
    gen_value = scatter_about(seeds[2], (D, HW), D ** -0.5, 0.078125, ((0, 2), (1, 4)))
    gen_head = scatter_about(seeds[3], (HW, C), HW ** -0.5, 0.125, ((0, 4),))
    critic_embed = scatter_about(seeds[4], (2, C, D), C ** -0.5, 0.75)
    critic_gain = jnp.clip(1.0 + 0.1 * jax.random.normal(seeds[5], (2, D), jnp.float32), 0.5, 1.5).astype(jnp.bfloat16)
    critic_value = scatter_about(seeds[6], (D, 2 * HW), D ** -0.5, 0.078125, ((0, 2), (1, 16)))
    critic_head = scatter_about(seeds[7], (2 * HW, C), HW ** -0.5, 0.125, ((0, 16),))
    noise = scatter_about(seeds[8], (TOKENS, C), 1.0, 6.0, ((0, 2),))
    owner = draw_owner(jax.random.fold_in(seeds[13], 71), 0)
    tsteps = jax.random.randint(seeds[10], (FRAMES,), 0, NT).astype(jnp.int32)
    noise_mix = jnp.clip(jax.random.uniform(seeds[11], (2, NT), jnp.float32, 0.3, 1.0), 0.3, 1.0)
    gap_weight = jnp.clip(jnp.exp(jax.random.uniform(seeds[12], (NT,), jnp.float32, math.log(2.0), math.log(16.0))), 2.0, 16.0)
    return {"hidden": hidden, "norm_gain": norm_gain, "gen_value": gen_value, "gen_head": gen_head, "critic_embed": critic_embed, "critic_gain": critic_gain, "critic_value": critic_value, "critic_head": critic_head, "noise": noise, "owner": owner, "tsteps": tsteps, "noise_mix": noise_mix, "gap_weight": gap_weight}


def gelu_tanh(v):
    return jax.nn.gelu(v, approximate=True)

def reference(hidden, norm_gain, gen_value, gen_head, critic_embed, critic_gain, critic_value, critic_head, noise, owner, tsteps, noise_mix, gap_weight):
    block = math.gcd(TOKENS, 2048)
    count = TOKENS // block
    cols = HW // N_TP
    gain = norm_gain.astype(jnp.float32)

    def gen_forward(rows):
        inputs = rows.astype(jnp.float32)
        inverse = lax.rsqrt(lax.optimization_barrier(jnp.mean(inputs * inputs, axis=-1, keepdims=True)) + 1e-06)
        normed = (inputs * inverse * gain).astype(jnp.bfloat16)
        values = jnp.dot(normed, gen_value, preferred_element_type=jnp.float32)
        activated = gelu_tanh(values).astype(jnp.bfloat16)
        total = jnp.zeros((rows.shape[0], C), jnp.float32)
        for part in range(N_TP):
            term = jnp.dot(activated[:, part * cols:(part + 1) * cols], gen_head[part * cols:(part + 1) * cols], preferred_element_type=jnp.float32)
            total = total + lax.optimization_barrier(term.astype(jnp.bfloat16)).astype(jnp.float32)
        return (total.astype(jnp.bfloat16), values)
    latent, values = lax.map(gen_forward, hidden.reshape(count, block, D))
    gen_latent = latent.reshape(TOKENS, C)
    placed = jnp.zeros((TOKENS, C), jnp.float32).at[owner].set(gen_latent.astype(jnp.float32))
    frame_at = jnp.zeros((TOKENS,), jnp.int32).at[owner].set(jnp.arange(TOKENS, dtype=jnp.int32) // FTOK)
    level = tsteps[frame_at]
    signal_part = noise_mix[0][level][:, None]
    noise_part = noise_mix[1][level][:, None]
    weight = gap_weight[level][:, None]
    noisy = (signal_part * placed + noise_part * noise.astype(jnp.float32)).astype(jnp.bfloat16)

    def critic_pass(noisy_rows):
        outputs = []
        for which in range(2):
            embedded = jnp.dot(noisy_rows, critic_embed[which], preferred_element_type=jnp.float32)
            scale_rows = lax.rsqrt(lax.optimization_barrier(jnp.mean(embedded * embedded, axis=-1, keepdims=True)) + 1e-06)
            critic_normed = (embedded * scale_rows * critic_gain[which].astype(jnp.float32)).astype(jnp.bfloat16)
            critic_values = jnp.dot(critic_normed, critic_value[:, which * HW:(which + 1) * HW], preferred_element_type=jnp.float32)
            critic_act = gelu_tanh(critic_values).astype(jnp.bfloat16)
            outputs.append(jnp.dot(critic_act, critic_head[which * HW:(which + 1) * HW], preferred_element_type=jnp.float32))
        return outputs[1] - outputs[0]
    gap = lax.map(critic_pass, noisy.reshape(count, block, C)).reshape(TOKENS, C)
    pull = (weight * gap).astype(jnp.bfloat16)
    cotangent = pull[owner]

    def gen_backward(items):
        rows, vals, cot = items
        inputs = rows.astype(jnp.float32)
        inverse = lax.rsqrt(lax.optimization_barrier(jnp.mean(inputs * inputs, axis=-1, keepdims=True)) + 1e-06)
        grad_act = lax.dot_general(cot, gen_head, (((1,), (1,)), ((), ())), preferred_element_type=jnp.float32)
        gelu_back = jax.vjp(gelu_tanh, vals)[1]
        grad_values = gelu_back(grad_act)[0].astype(jnp.bfloat16)
        total = jnp.zeros((rows.shape[0], D), jnp.float32)
        for part in range(N_TP):
            term = lax.dot_general(grad_values[:, part * cols:(part + 1) * cols], gen_value[:, part * cols:(part + 1) * cols], (((1,), (1,)), ((), ())), preferred_element_type=jnp.float32)
            total = total + lax.optimization_barrier(term.astype(jnp.bfloat16)).astype(jnp.float32)
        scaled = total * gain
        mixed = lax.optimization_barrier(jnp.mean(inputs * scaled, axis=-1, keepdims=True))
        return (inverse * scaled - inputs * inverse * inverse * inverse * mixed).astype(jnp.bfloat16)
    grad_hidden = lax.map(gen_backward, (hidden.reshape(count, block, D), values.reshape(count, block, HW), cotangent.reshape(count, block, C)))
    return (gen_latent, grad_hidden.reshape(TOKENS, D))
```

```python
import jax
import jax.numpy as jnp
from jax import lax
from jax.sharding import PartitionSpec as P

FTOK = 2048


def gelu_tanh(v):
    return jax.nn.gelu(v, approximate=True)


def split_bf16(v):
    hi = lax.reduce_precision(v, 8, 7)
    return hi.astype(jnp.bfloat16), (v - hi).astype(jnp.bfloat16)


def local(
    hidden,
    norm_gain,
    gen_value,
    gen_head,
    critic_embed,
    critic_gain,
    critic_value,
    critic_head,
    noise,
    owner,
    tsteps,
    noise_mix,
    gap_weight,
):
    f32 = jnp.float32
    rows, width = hidden.shape
    depth = gen_value.shape[0]
    seq_count = lax.axis_size("seq")
    group_count = lax.axis_size("group")
    tp_count = lax.axis_size("tp")
    group_id = lax.axis_index("group")
    seq_id = lax.axis_index("seq")
    tp_id = lax.axis_index("tp")
    critic_id = group_id // (group_count // 2)
    frame = ((group_id * seq_count + seq_id) * rows) // FTOK
    level = lax.dynamic_index_in_dim(tsteps, frame, 0, keepdims=False)
    mix = lax.dynamic_index_in_dim(noise_mix, level, 1, keepdims=False)
    weight = lax.dynamic_index_in_dim(gap_weight, level, 0, keepdims=False)

    gen_full = lax.all_gather(gen_value, "seq", axis=0, tiled=True)
    noise_rows = lax.all_gather(noise, "seq", axis=0, tiled=True)[owner].astype(f32)

    first = seq_id * depth
    embed = lax.dynamic_slice(critic_embed, (critic_id, 0, first), (1, critic_embed.shape[1], depth))[0]
    gains = lax.dynamic_slice(critic_gain, (critic_id, first), (1, depth))
    eg_hi, eg_lo = split_bf16(embed.astype(f32) * gains.astype(f32))
    folded = jnp.dot(eg_hi, critic_value, preferred_element_type=f32) + jnp.dot(
        eg_lo, critic_value, preferred_element_type=f32
    )
    folded = lax.psum(folded, "seq")
    m_hi, m_lo = split_bf16(folded)
    m_pair = jnp.concatenate([m_hi, m_lo], axis=0)
    m_all = lax.all_gather(m_pair, "group", axis=0, tiled=False)
    head_all = lax.all_gather(critic_head, "group", axis=0, tiled=False)

    inputs = hidden.astype(f32)
    inverse = lax.rsqrt(jnp.mean(inputs * inputs, axis=-1, keepdims=True) + 1e-06)
    gain = norm_gain.astype(f32)
    normed = (inputs * inverse * gain).astype(jnp.bfloat16)
    values = jnp.dot(normed, gen_full, preferred_element_type=f32)
    activated, gelu_back = jax.vjp(gelu_tanh, values)
    latent_part = jnp.dot(activated.astype(jnp.bfloat16), gen_head, preferred_element_type=f32)
    gen_latent = lax.psum(latent_part.astype(jnp.bfloat16), "tp")

    noisy = (mix[0] * gen_latent.astype(f32) + mix[1] * noise_rows).astype(jnp.bfloat16)
    noisy32 = noisy.astype(f32)
    pair = jnp.concatenate([noisy, noisy], axis=1)
    scales = []
    for which in range(2):
        gram = lax.dot_general(
            critic_embed[which], critic_embed[which], (((1,), (1,)), ((), ())), preferred_element_type=f32
        )
        quad = jnp.sum(jnp.dot(noisy32, gram, precision=lax.Precision.HIGHEST) * noisy32, axis=-1, keepdims=True)
        scales.append(lax.rsqrt(jnp.maximum(quad, 0.0) / width + 1e-06))
    gap = 0.0
    for member in range(group_count):
        which = member // (group_count // 2)
        crit = jnp.dot(pair, m_all[member], preferred_element_type=f32) * scales[which]
        term = jnp.dot(gelu_tanh(crit).astype(jnp.bfloat16), head_all[member], preferred_element_type=f32)
        gap = gap + term if which else gap - term
    gap = lax.psum(gap.astype(jnp.bfloat16), "tp").astype(f32)
    cotangent = (weight * gap).astype(jnp.bfloat16)

    grad_act = lax.dot_general(cotangent, gen_head, (((1,), (1,)), ((), ())), preferred_element_type=f32)
    grad_values = gelu_back(grad_act)[0].astype(jnp.bfloat16)
    inner = jnp.sum(grad_values.astype(f32) * values, axis=-1, keepdims=True)
    mixed = lax.psum(inner, "tp") / (inverse * width)
    grad_part = lax.dot_general(grad_values, gen_full, (((1,), (1,)), ((), ())), preferred_element_type=f32)
    grad_normed = lax.psum_scatter(grad_part.astype(jnp.bfloat16), "tp", scatter_dimension=1, tiled=True)
    columns = width // tp_count
    own = lax.dynamic_slice_in_dim(hidden, tp_id * columns, columns, 1).astype(f32)
    own_gain = lax.dynamic_slice_in_dim(gain, tp_id * columns, columns, 0)
    scaled = grad_normed.astype(f32) * own_gain
    grad_hidden = inverse * scaled - own * inverse * inverse * inverse * mixed
    return (gen_latent, grad_hidden.astype(jnp.bfloat16))


def solution(mesh):
    return jax.shard_map(
        local,
        mesh=mesh,
        in_specs=(
            P(("group", "seq"), None),
            P(),
            P("seq", "tp"),
            P("tp", None),
            P(),
            P(),
            P("seq", ("group", "tp")),
            P(("group", "tp"), None),
            P("seq", None),
            P(("group", "seq")),
            P(),
            P(),
            P(),
        ),
        out_specs=(P(("group", "seq"), None), P(("group", "seq"), "tp")),
        check_vma=False,
    )
```

```python
import functools
import jax
import jax.numpy as jnp
from jax import lax
from jax.experimental import pallas as pl
from jax.experimental.pallas import tpu as pltpu
from jax.sharding import PartitionSpec as P

FTOK = 2048
MESH = pl.DeviceIdType.MESH
F32 = jnp.float32
BF16 = jnp.bfloat16
ROOT = 0.7978845608028654
CUBE = 0.044715


def split_bf16(v):
    hi = lax.reduce_precision(v, 8, 7)
    return hi.astype(BF16), (v - hi).astype(BF16)


def gelu_tanh(v):
    return 0.5 * v * (1.0 + jnp.tanh(ROOT * (v + CUBE * v * v * v)))


def dot(a, b):
    return jnp.dot(a, b, preferred_element_type=F32)


def dot_t(a, b):
    return lax.dot_general(a, b, (((1,), (1,)), ((), ())), preferred_element_type=F32)


def kernel(
    ng, ns, nt, shared, pieces,
    hidden, gain, weights, gen_head, embed, eg_pair, crit_value, crit_head, noise, owner, coef,
    latent_out, grad_out,
    wall, normed, inv_ref, values, slope, mpart, mall, hall, noise_all, latp, gapp, inn,
    send_r, send_l, recv_r, recv_l, total,
    own_sem, w_send, w_recv, f_send, f_recv, m_send, m_recv, n_send, n_recv,
    g_send, g_recv, h_send, h_recv, t_send, t_recv, rs_sem, rr_sem, ls_sem, lr_sem,
):
    g = lax.axis_index("group")
    s = lax.axis_index("seq")
    t = lax.axis_index("tp")
    rows, width = hidden.shape
    depth = weights.shape[0]
    crit_rows = noise.shape[0]
    columns = width // nt
    pending = []

    def seq_peer(o):
        return lax.rem(s + o, ns)

    def group_peer(o):
        return lax.rem(g + o, ng)

    def tp_peer(o):
        return lax.rem(t + o, nt)

    def push(src, dst, send, recv, where):
        copy = pltpu.make_async_remote_copy(
            src_ref=src, dst_ref=dst, send_sem=send, recv_sem=recv,
            device_id=where, device_id_type=MESH,
        )
        copy.start()
        pending.append(copy)
        return copy

    barrier = pltpu.get_barrier_semaphore()
    for o in range(1, ns):
        pl.semaphore_signal(barrier, inc=1, device_id={"seq": seq_peer(o)}, device_id_type=MESH)
    for o in range(1, ng):
        pl.semaphore_signal(barrier, inc=1, device_id={"group": group_peer(o)}, device_id_type=MESH)
    for o in range(1, nt):
        pl.semaphore_signal(barrier, inc=1, device_id={"tp": tp_peer(o)}, device_id_type=MESH)
    pl.semaphore_wait(barrier, ns + ng + nt - 3)

    local = pltpu.make_async_copy(weights, wall.at[pl.ds(s * depth, depth), :], own_sem)
    local.start()
    quarter = depth // ng if shared else depth
    step = quarter // pieces
    mine = g * quarter if shared else 0
    w_copies = {}
    for p in range(pieces):
        for o in range(1, ns):
            w_copies[o, p] = push(
                weights.at[pl.ds(mine + p * step, step), :],
                wall.at[pl.ds(s * depth + mine + p * step, step), :],
                w_send.at[o - 1, p], w_recv.at[o - 1, p], {"seq": seq_peer(o)},
            )
    n_copies = [
        push(noise, noise_all.at[s], n_send.at[o - 1], n_recv.at[o - 1], {"seq": seq_peer(o)})
        for o in range(1, ns)
    ]
    h_copies = [
        push(crit_head, hall.at[g], h_send.at[o - 1], h_recv.at[o - 1], {"group": group_peer(o)})
        for o in range(1, ng)
    ]
    noise_all[s] = noise[...]
    hall[g] = crit_head[...]

    folded = dot(eg_pair[...], crit_value[...])
    half = folded.shape[0] // 2
    mpart[s] = folded[:half] + folded[half:]
    m_copies = [
        push(mpart.at[s], mpart.at[s], m_send.at[o - 1], m_recv.at[o - 1], {"seq": seq_peer(o)})
        for o in range(1, ns)
    ]

    def norm_rows(r, carry):
        at = pl.ds(pl.multiple_of(r * 32, 32), 32)
        x = hidden[at, :].astype(F32)
        inverse = lax.rsqrt(jnp.mean(x * x, axis=-1, keepdims=True) + 1e-06)
        normed[at, :] = (x * inverse * gain[...].astype(F32)).astype(BF16)
        inv_ref[at, :] = jnp.broadcast_to(inverse, (32, 128))
        return carry

    lax.fori_loop(0, rows // 32, norm_rows, 0)
    values[...] = jnp.zeros_like(values)

    def add_rows(start, size):
        at = pl.multiple_of(start, 128)
        values[...] += dot(normed[:, pl.ds(at, size)], wall[pl.ds(at, size), :])

    if shared:
        x_copies, c_copies, d_copies = {}, {}, {}
        for p in range(pieces):
            for o in range(1, ns):
                w_copies[o, p].wait_recv()
                base = lax.rem(s - o + ns, ns) * depth
                at = pl.ds(base + mine + p * step, step)
                x_copies[o, p] = push(
                    wall.at[at, :], wall.at[at, :],
                    f_send.at[0, o - 1, p], f_recv.at[0, o - 1, p], {"group": g ^ 2},
                )
                c_copies[o, p] = push(
                    wall.at[at, :], wall.at[at, :],
                    f_send.at[1, o - 1, p], f_recv.at[1, o - 1, p], {"group": g ^ 1},
                )
            if p == 0:
                local.wait()

                def own_rows(j, carry):
                    add_rows(s * depth + j * quarter, quarter)
                    return carry

                lax.fori_loop(0, ng, own_rows, 0)
        for p in range(pieces):
            for o in range(1, ns):
                x_copies[o, p].wait_recv()
                base = lax.rem(s - o + ns, ns) * depth
                at = pl.ds(base + (g ^ 2) * quarter + p * step, step)
                d_copies[o, p] = push(
                    wall.at[at, :], wall.at[at, :],
                    f_send.at[2, o - 1, p], f_recv.at[2, o - 1, p], {"group": g ^ 1},
                )
    else:
        local.wait()

    for copy in m_copies:
        copy.wait_recv()
    whole = mpart[0]
    for k in range(1, ns):
        whole = whole + mpart[k]
    high = whole.astype(BF16)
    mall[g, :half] = high
    mall[g, half:] = (whole - high.astype(F32)).astype(BF16)
    g_copies = [
        push(mall.at[g], mall.at[g], g_send.at[o - 1], g_recv.at[o - 1], {"group": group_peer(o)})
        for o in range(1, ng)
    ]
    grams = []
    for which in range(2):
        gram = dot_t(embed[which], embed[which])
        first = gram.astype(BF16)
        rest = gram - first.astype(F32)
        second = rest.astype(BF16)
        grams.append((first, second, (rest - second.astype(F32)).astype(BF16)))
    for copy in n_copies:
        copy.wait_recv()

    def pick(k, carry):
        place = lax.broadcasted_iota(jnp.int32, (rows, crit_rows), 1) + k * crit_rows
        hot = (place == owner[...]).astype(F32).astype(BF16)
        return carry + dot(hot, noise_all[k])

    noise_rows = lax.fori_loop(0, ns, pick, jnp.zeros((rows, noise.shape[1]), F32))

    if shared:
        for o in range(1, ns):
            base = lax.rem(s - o + ns, ns) * depth
            add_rows(base + g * quarter, quarter)
            add_rows(base + (g ^ 2) * quarter, quarter)
            for p in range(pieces):
                c_copies[o, p].wait_recv()
            add_rows(base + (g ^ 1) * quarter, quarter)
            for p in range(pieces):
                d_copies[o, p].wait_recv()
            add_rows(base + (g ^ 3) * quarter, quarter)
    else:
        for copy in w_copies.values():
            copy.wait_recv()

        def all_rows(j, carry):
            add_rows(j * (width // 8), width // 8)
            return carry

        lax.fori_loop(0, 8, all_rows, 0)

    def share_tp(buffer, index):
        return [
            push(buffer.at[t], buffer.at[t], t_send.at[index, o - 1], t_recv.at[index, o - 1], {"tp": tp_peer(o)})
            for o in range(1, nt)
        ]

    def sum_tp(buffer, copies):
        for copy in copies:
            copy.wait_recv()
        out = buffer[0].astype(F32)
        for k in range(1, nt):
            out = out + buffer[k].astype(F32)
        return out

    v = values[...]
    tanh = jnp.tanh(ROOT * (v + CUBE * v * v * v))
    latp[t] = dot((0.5 * v * (1.0 + tanh)).astype(BF16), gen_head[...]).astype(BF16)
    lat_copies = share_tp(latp, 0)
    slope[...] = 0.5 * (1.0 + tanh) + 0.5 * v * (1.0 - tanh * tanh) * ROOT * (1.0 + 3.0 * CUBE * v * v)
    for copy in g_copies + h_copies:
        copy.wait_recv()
    latent = sum_tp(latp, lat_copies).astype(BF16)
    latent_out[...] = latent

    noisy = (coef[:, 0:1] * latent.astype(F32) + coef[:, 1:2] * noise_rows).astype(BF16)
    noisy32 = noisy.astype(F32)
    scales = []
    for which in range(2):
        a, b, c = grams[which]
        quad = jnp.sum((dot(noisy, a) + dot(noisy, b) + dot(noisy, c)) * noisy32, axis=-1, keepdims=True)
        scales.append(lax.rsqrt(jnp.maximum(quad, 0.0) / width + 1e-06))
    pair = jnp.concatenate([noisy, noisy], axis=1)
    gap = jnp.zeros((rows, noise.shape[1]), F32)
    for member in range(ng):
        which = member // (ng // 2)
        act = gelu_tanh(dot(pair, mall[member]) * scales[which]).astype(BF16)
        term = dot(act, hall[member])
        gap = gap + term if which else gap - term
    gapp[t] = gap.astype(BF16)
    gap = sum_tp(gapp, share_tp(gapp, 1))
    cotangent = (coef[:, 2:3] * gap).astype(BF16)

    grad_values = (slope[...] * dot_t(cotangent, gen_head[...])).astype(BF16)
    inner = jnp.sum(grad_values.astype(F32) * values[...], axis=-1, keepdims=True)
    inn[t] = jnp.broadcast_to(inner, (rows, 128)).T[:8]
    inn_copies = share_tp(inn, 2)

    block = 256 if columns % 256 == 0 else columns

    def part(q, out, extra):
        def one(j, carry):
            at = pl.ds(pl.multiple_of(j * block, block), block)
            w = wall[pl.ds(pl.multiple_of(q * columns + j * block, block), block), :]
            term = dot_t(grad_values, w)
            if extra is not None:
                term = term + extra[:, at].astype(F32)
            out[:, at] = term.astype(out.dtype)
            return carry

        lax.fori_loop(0, columns // block, one, 0)

    def chain(d, to_right):
        buf_s, buf_r = (send_r, recv_r) if to_right else (send_l, recv_l)
        sem_s, sem_r = (rs_sem, rr_sem) if to_right else (ls_sem, lr_sem)
        target = t + d if to_right else t - d
        inside = target <= nt - 1 if to_right else target >= 0
        starts = t == 0 if to_right else t == nt - 1
        neighbour = {"tp": t + 1 if to_right else t - 1}

        def link(k):
            return pltpu.make_async_remote_copy(
                src_ref=buf_s.at[k], dst_ref=buf_r.at[k], send_sem=sem_s.at[k], recv_sem=sem_r.at[k],
                device_id=neighbour, device_id_type=MESH,
            )

        @pl.when(inside)
        def _():
            if d < nt - 1:
                @pl.when(starts)
                def _():
                    part(target, buf_s.at[d - 1], None)
                    link(d).wait_send()

                @pl.when(jnp.logical_not(starts))
                def _():
                    link(d).wait_recv()
                    part(target, buf_s.at[d - 1], buf_r.at[d])
                    if d < nt - 2:
                        @pl.when(target + 1 <= nt - 1 if to_right else target - 1 >= 0)
                        def _():
                            link(d).wait_send()
            else:
                part(target, buf_s.at[d - 1], None)
            link(d - 1).start()

    def chain_end(to_right):
        buf_s, buf_r = (send_r, recv_r) if to_right else (send_l, recv_l)
        sem_s, sem_r = (rs_sem, rr_sem) if to_right else (ls_sem, lr_sem)
        neighbour = {"tp": t + 1 if to_right else t - 1}
        link = pltpu.make_async_remote_copy(
            src_ref=buf_s.at[0], dst_ref=buf_r.at[0], send_sem=sem_s.at[0], recv_sem=sem_r.at[0],
            device_id=neighbour, device_id_type=MESH,
        )

        @pl.when(t > 0 if to_right else t < nt - 1)
        def _():
            link.wait_recv()
            total[...] += buf_r[0].astype(F32)

        @pl.when(t < nt - 1 if to_right else t > 0)
        def _():
            link.wait_send()

    for d in range(nt - 1, 0, -1):
        chain(d, True)
        chain(d, False)
    part(t, total, None)
    inner_all = sum_tp(inn, inn_copies)
    inner_col = jnp.broadcast_to(inner_all[0:1], (128, rows)).T[:, :1]
    chain_end(True)
    chain_end(False)
    inverse = inv_ref[:, :1]
    mixed = inner_col / (inverse * width)
    factor = inverse * inverse * inverse * mixed

    def finish(j, carry):
        at = pl.ds(pl.multiple_of(j * block, block), block)
        far = pl.ds(pl.multiple_of(t * columns + j * block, block), block)
        scaled = total[:, at] * gain[:, far].astype(F32)
        grad_out[:, at] = (inverse * scaled - hidden[:, far].astype(F32) * factor).astype(BF16)
        return carry

    lax.fori_loop(0, columns // block, finish, 0)
    for copy in pending:
        copy.wait_send()


def local(
    hidden,
    norm_gain,
    gen_value,
    gen_head,
    critic_embed,
    critic_gain,
    critic_value,
    critic_head,
    noise,
    owner,
    tsteps,
    noise_mix,
    gap_weight,
):
    rows, width = hidden.shape
    depth, heads = gen_value.shape
    crit_rows, latent_width = noise.shape
    crit_cols = critic_value.shape[1]
    ns = lax.axis_size("seq")
    ng = lax.axis_size("group")
    nt = lax.axis_size("tp")
    group_id = lax.axis_index("group")
    seq_id = lax.axis_index("seq")
    critic_id = group_id // (ng // 2)
    frame = ((group_id * ns + seq_id) * rows) // FTOK
    level = lax.dynamic_index_in_dim(tsteps, frame, 0, keepdims=False)
    mix = lax.dynamic_index_in_dim(noise_mix, level, 1, keepdims=False)
    weight = lax.dynamic_index_in_dim(gap_weight, level, 0, keepdims=True)
    coef = jnp.pad(jnp.concatenate([mix, weight]), (0, 125)).reshape(1, 128)
    first = seq_id * depth
    embed = lax.dynamic_slice(critic_embed, (critic_id, 0, first), (1, latent_width, depth))[0]
    gains = lax.dynamic_slice(critic_gain, (critic_id, first), (1, depth))
    eg_pair = jnp.concatenate(split_bf16(embed.astype(F32) * gains.astype(F32)), axis=0)

    shared = ng == 4 and depth % (128 * ng) == 0
    pieces = 4 if shared else 1
    vmem = pl.BlockSpec(memory_space=pltpu.VMEM)
    columns = width // nt
    dma = pltpu.SemaphoreType.DMA
    return pl.pallas_call(
        functools.partial(kernel, ng, ns, nt, shared, pieces),
        out_shape=(
            jax.ShapeDtypeStruct((rows, latent_width), BF16),
            jax.ShapeDtypeStruct((rows, columns), BF16),
        ),
        in_specs=[vmem, vmem, pl.BlockSpec(memory_space=pl.ANY)] + [vmem] * 8,
        out_specs=(vmem, vmem),
        scratch_shapes=[
            pltpu.VMEM((width, heads), BF16),
            pltpu.VMEM((rows, width), BF16),
            pltpu.VMEM((rows, 128), F32),
            pltpu.VMEM((rows, heads), F32),
            pltpu.VMEM((rows, heads), F32),
            pltpu.VMEM((ns, latent_width, crit_cols), F32),
            pltpu.VMEM((ng, 2 * latent_width, crit_cols), BF16),
            pltpu.VMEM((ng, crit_cols, latent_width), BF16),
            pltpu.VMEM((ns, crit_rows, latent_width), BF16),
            pltpu.VMEM((nt, rows, latent_width), BF16),
            pltpu.VMEM((nt, rows, latent_width), BF16),
            pltpu.VMEM((nt, 8, rows), F32),
            pltpu.VMEM((nt - 1, rows, columns), BF16),
            pltpu.VMEM((nt - 1, rows, columns), BF16),
            pltpu.VMEM((nt - 1, rows, columns), BF16),
            pltpu.VMEM((nt - 1, rows, columns), BF16),
            pltpu.VMEM((rows, columns), F32),
            dma,
            dma((ns - 1, pieces)),
            dma((ns - 1, pieces)),
            dma((3, ns - 1, pieces)),
            dma((3, ns - 1, pieces)),
            dma((ns - 1,)),
            dma((ns - 1,)),
            dma((ns - 1,)),
            dma((ns - 1,)),
            dma((ng - 1,)),
            dma((ng - 1,)),
            dma((ng - 1,)),
            dma((ng - 1,)),
            dma((3, nt - 1)),
            dma((3, nt - 1)),
            dma((nt - 1,)),
            dma((nt - 1,)),
            dma((nt - 1,)),
            dma((nt - 1,)),
        ],
        compiler_params=pltpu.CompilerParams(
            collective_id=0, has_side_effects=True, vmem_limit_bytes=56 * 1024 * 1024
        ),
    )(
        hidden, norm_gain.reshape(1, width), gen_value, gen_head, critic_embed, eg_pair,
        critic_value, critic_head, noise, owner.reshape(rows, 1), coef,
    )


def solution(mesh):
    return jax.shard_map(
        local,
        mesh=mesh,
        in_specs=(
            P(("group", "seq"), None),
            P(),
            P("seq", "tp"),
            P("tp", None),
            P(),
            P(),
            P("seq", ("group", "tp")),
            P(("group", "tp"), None),
            P("seq", None),
            P(("group", "seq")),
            P(),
            P(),
            P(),
        ),
        out_specs=(P(("group", "seq"), None), P(("group", "seq"), "tp")),
        check_vma=False,
    )
```

```python
import functools
import jax
import jax.numpy as jnp
from jax import lax
from jax.experimental import pallas as pl
from jax.experimental.pallas import tpu as pltpu
from jax.sharding import PartitionSpec as P

FTOK = 2048
HALVES = 2
MESH = pl.DeviceIdType.MESH
F32 = jnp.float32
BF16 = jnp.bfloat16
ROOT = 0.7978845608028654
CUBE = 0.044715


def split_bf16(v):
    hi = lax.reduce_precision(v, 8, 7)
    return hi.astype(BF16), (v - hi).astype(BF16)


def gelu_tanh(v):
    return 0.5 * v * (1.0 + jnp.tanh(ROOT * (v + CUBE * v * v * v)))


def dot(a, b):
    return jnp.dot(a, b, preferred_element_type=F32)


def dot_t(a, b):
    return lax.dot_general(a, b, (((1,), (1,)), ((), ())), preferred_element_type=F32)


def kernel(
    ng, ns, nt, shared, pieces,
    hidden, gain_in, weights, gen_head, embed, scaling, crit_value, crit_head, noise, owner, tsteps, tables, weighting,
    latent_out, grad_out,
    gain, wall, normed, inv_ref, values, slope, mpart, mall, hall, noise_all, latp, gapp, inn,
    send_r, send_l, recv_r, recv_l, total,
    own_sem, w_send, w_recv, f_send, f_recv, m_send, m_recv, n_send, n_recv,
    g_send, g_recv, h_send, h_recv, t_send, t_recv, rs_sem, rr_sem, ls_sem, lr_sem,
):
    g = lax.axis_index("group")
    s = lax.axis_index("seq")
    t = lax.axis_index("tp")
    rows, width = hidden.shape
    depth = weights.shape[0]
    crit_rows = noise.shape[1]
    channels = noise.shape[0]
    columns = width // nt
    pending = []

    def seq_peer(o):
        return lax.rem(s + o, ns)

    def group_peer(o):
        return lax.rem(g + o, ng)

    def tp_peer(o):
        return lax.rem(t + o, nt)

    def push(src, dst, send, recv, where):
        copy = pltpu.make_async_remote_copy(
            src_ref=src, dst_ref=dst, send_sem=send, recv_sem=recv,
            device_id=where, device_id_type=MESH,
        )
        copy.start()
        pending.append(copy)
        return copy

    barrier = pltpu.get_barrier_semaphore()
    for o in range(1, ns):
        pl.semaphore_signal(barrier, inc=1, device_id={"seq": seq_peer(o)}, device_id_type=MESH)
    for o in range(1, ng):
        pl.semaphore_signal(barrier, inc=1, device_id={"group": group_peer(o)}, device_id_type=MESH)
    for o in range(1, nt):
        pl.semaphore_signal(barrier, inc=1, device_id={"tp": tp_peer(o)}, device_id_type=MESH)
    pl.semaphore_wait(barrier, ns + ng + nt - 3)

    local = pltpu.make_async_copy(weights, wall.at[pl.ds(s * depth, depth), :], own_sem)
    local.start()
    quarter = depth // ng if shared else depth
    step = quarter // pieces
    mine = g * quarter if shared else 0
    w_copies = {}
    for p in range(pieces):
        for o in range(1, ns):
            w_copies[o, p] = push(
                weights.at[pl.ds(mine + p * step, step), :],
                wall.at[pl.ds(s * depth + mine + p * step, step), :],
                w_send.at[o - 1, p], w_recv.at[o - 1, p], {"seq": seq_peer(o)},
            )
    n_copies = [
        push(noise, noise_all.at[s], n_send.at[o - 1], n_recv.at[o - 1], {"seq": seq_peer(o)})
        for o in range(1, ns)
    ]
    h_copies = [
        push(crit_head, hall.at[g], h_send.at[o - 1], h_recv.at[o - 1], {"group": group_peer(o)})
        for o in range(1, ng)
    ]
    noise_all[s] = noise[...]
    hall[g] = crit_head[...]

    half = channels
    if depth % 128 == 0:
        critic = g // (ng // 2)
        at = pl.ds(pl.multiple_of(s * depth, 128), depth)
        both = scaling[:, at].astype(F32)
        eg = embed[critic, :, at].astype(F32) * jnp.where(critic == 0, both[0:1], both[1:2])
        eg_high = eg.astype(BF16)
        eg_low = (eg - eg_high.astype(F32)).astype(BF16)
        eg_pair = jnp.concatenate([eg_high, eg_low], axis=0)
    else:
        eg_pair = scaling[...]
    folded = dot_t(eg_pair, crit_value[...])
    mpart[s] = folded[:half] + folded[half:]
    m_copies = [
        push(mpart.at[s], mpart.at[s], m_send.at[o - 1], m_recv.at[o - 1], {"seq": seq_peer(o)})
        for o in range(1, ns)
    ]

    gain[...] = gain_in[...].astype(F32).reshape(1, width)

    def norm_rows(r, carry):
        at = pl.ds(pl.multiple_of(r * 32, 32), 32)
        x = hidden[at, :].astype(F32)
        inverse = lax.rsqrt(jnp.mean(x * x, axis=-1, keepdims=True) + 1e-06)
        normed[at, :] = (x * inverse * gain[...]).astype(BF16)
        inv_ref[at, :] = jnp.broadcast_to(inverse, (32, 128))
        return carry

    lax.fori_loop(0, rows // 32, norm_rows, 0)
    values[...] = jnp.zeros_like(values)

    def add_rows(start, size):
        at = pl.multiple_of(start, 128)
        values[...] += dot(normed[:, pl.ds(at, size)], wall[pl.ds(at, size), :])

    if shared:
        x_copies, c_copies, d_copies = {}, {}, {}
        for p in range(pieces):
            for o in range(1, ns):
                w_copies[o, p].wait_recv()
                base = lax.rem(s - o + ns, ns) * depth
                at = pl.ds(base + mine + p * step, step)
                x_copies[o, p] = push(
                    wall.at[at, :], wall.at[at, :],
                    f_send.at[0, o - 1, p], f_recv.at[0, o - 1, p], {"group": g ^ 2},
                )
                c_copies[o, p] = push(
                    wall.at[at, :], wall.at[at, :],
                    f_send.at[1, o - 1, p], f_recv.at[1, o - 1, p], {"group": g ^ 1},
                )
            if p == 0:
                local.wait()

                def own_rows(j, carry):
                    add_rows(s * depth + j * quarter, quarter)
                    return carry

                lax.fori_loop(0, ng, own_rows, 0)
        for p in range(pieces):
            for o in range(1, ns):
                x_copies[o, p].wait_recv()
                base = lax.rem(s - o + ns, ns) * depth
                at = pl.ds(base + (g ^ 2) * quarter + p * step, step)
                d_copies[o, p] = push(
                    wall.at[at, :], wall.at[at, :],
                    f_send.at[2, o - 1, p], f_recv.at[2, o - 1, p], {"group": g ^ 1},
                )
    else:
        local.wait()

    for copy in m_copies:
        copy.wait_recv()
    whole = mpart[0]
    for k in range(1, ns):
        whole = whole + mpart[k]
    high = whole.astype(BF16)
    high32 = high.astype(F32)
    cols = whole.shape[1]
    fill = -cols % 128
    both = jnp.concatenate([high32, whole - high32], axis=0)
    if fill:
        both = jnp.concatenate([both, jnp.zeros((2 * half, fill), F32)], axis=1)
    mall[g] = both.T[:cols].astype(BF16)
    g_copies = [
        push(mall.at[g], mall.at[g], g_send.at[o - 1], g_recv.at[o - 1], {"group": group_peer(o)})
        for o in range(1, ng)
    ]
    grams = []
    for which in range(2):
        gram = dot_t(embed[which], embed[which])
        first = gram.astype(BF16)
        rest = gram - first.astype(F32)
        second = rest.astype(BF16)
        grams.append((first, second, (rest - second.astype(F32)).astype(BF16)))
    for copy in n_copies:
        copy.wait_recv()

    def pick(k, carry):
        place = lax.broadcasted_iota(jnp.int32, (crit_rows, rows), 0) + k * crit_rows
        hot = jnp.where(place == owner_row, 1.0, 0.0).astype(BF16)
        return carry + dot(noise_all[k], hot)

    owner_row = owner[...].reshape(1, rows)
    noise_rows = lax.fori_loop(0, ns, pick, jnp.zeros((channels, rows), F32))
    level = tsteps[((g * ns + s) * rows) // FTOK]
    levels = tables.shape[1]
    found = lax.broadcasted_iota(jnp.int32, (1, levels), 1) == level
    mix = jnp.sum(jnp.where(found, tables[...], 0.0), axis=1, keepdims=True)
    weight = jnp.sum(jnp.where(found, weighting[...].reshape(1, levels), 0.0), axis=1, keepdims=True)

    if shared:
        for o in range(1, ns):
            base = lax.rem(s - o + ns, ns) * depth
            add_rows(base + g * quarter, quarter)
            add_rows(base + (g ^ 2) * quarter, quarter)
            for p in range(pieces):
                c_copies[o, p].wait_recv()
            add_rows(base + (g ^ 1) * quarter, quarter)
            for p in range(pieces):
                d_copies[o, p].wait_recv()
            add_rows(base + (g ^ 3) * quarter, quarter)
    else:
        for copy in w_copies.values():
            copy.wait_recv()

        def all_rows(j, carry):
            add_rows(j * (width // 8), width // 8)
            return carry

        lax.fori_loop(0, 8, all_rows, 0)

    def share_tp(buffer, index):
        return [
            push(buffer.at[t], buffer.at[t], t_send.at[index, o - 1], t_recv.at[index, o - 1], {"tp": tp_peer(o)})
            for o in range(1, nt)
        ]

    def sum_tp(buffer, copies):
        for copy in copies:
            copy.wait_recv()
        out = buffer[0].astype(F32)
        for k in range(1, nt):
            out = out + buffer[k].astype(F32)
        return out

    v = values[...]
    tanh = jnp.tanh(ROOT * (v + CUBE * v * v * v))
    latp[t] = dot_t(gen_head[...], (0.5 * v * (1.0 + tanh)).astype(BF16)).astype(BF16)
    lat_copies = share_tp(latp, 0)
    slope[...] = 0.5 * (1.0 + tanh) + 0.5 * v * (1.0 - tanh * tanh) * ROOT * (1.0 + 3.0 * CUBE * v * v)
    for copy in g_copies + h_copies:
        copy.wait_recv()
    latent = sum_tp(latp, lat_copies).astype(BF16)
    latent_out[...] = latent

    noisy = (mix[0:1] * latent.astype(F32) + mix[1:2] * noise_rows).astype(BF16)
    noisy32 = noisy.astype(F32)
    scales = []
    for which in range(2):
        a, b, c = grams[which]
        quad = jnp.sum((dot(a, noisy) + dot(b, noisy) + dot(c, noisy)) * noisy32, axis=0, keepdims=True)
        scales.append(lax.rsqrt(jnp.maximum(quad, 0.0) / width + 1e-06))
    pair = jnp.concatenate([noisy, noisy], axis=0)
    gap = jnp.zeros((channels, rows), F32)
    for member in range(ng):
        which = member // (ng // 2)
        act = gelu_tanh(dot(mall[member], pair) * scales[which]).astype(BF16)
        term = dot(hall[member], act)
        gap = gap + term if which else gap - term
    gapp[t] = gap.astype(BF16)
    gap = sum_tp(gapp, share_tp(gapp, 1))
    pull = weight * gap
    fill = -channels % 128
    if fill:
        pull = jnp.concatenate([pull, jnp.zeros((fill, rows), F32)], axis=0)
    cotangent = pull.T[:, :channels].astype(BF16)

    grad_values = (slope[...] * dot(cotangent, gen_head[...])).astype(BF16)
    inner = jnp.sum(grad_values.astype(F32) * values[...], axis=-1, keepdims=True)
    inn[t] = jnp.broadcast_to(inner, (rows, 128)).T[:8]
    inn_copies = share_tp(inn, 2)

    block = 256 if columns % 256 == 0 else columns
    part_rows = rows // HALVES

    def part(q, h, out, extra):
        lhs = grad_values[h * part_rows:(h + 1) * part_rows]

        def one(j, carry):
            at = pl.ds(pl.multiple_of(j * block, block), block)
            w = wall[pl.ds(pl.multiple_of(q * columns + j * block, block), block), :]
            term = dot_t(lhs, w)
            if extra is not None:
                term = term + extra[:, at].astype(F32)
            out[:, at] = term.astype(out.dtype)
            return carry

        lax.fori_loop(0, columns // block, one, 0)

    def linker(to_right):
        buf_s, buf_r = (send_r, recv_r) if to_right else (send_l, recv_l)
        sem_s, sem_r = (rs_sem, rr_sem) if to_right else (ls_sem, lr_sem)

        def link(k, h):
            return pltpu.make_async_remote_copy(
                src_ref=buf_s.at[k, h], dst_ref=buf_r.at[k, h], send_sem=sem_s.at[k, h], recv_sem=sem_r.at[k, h],
                device_id={"tp": t + 1 if to_right else t - 1}, device_id_type=MESH,
            )

        return buf_s, buf_r, link

    def chain(d, h, to_right):
        buf_s, buf_r, link = linker(to_right)
        target = t + d if to_right else t - d
        inside = target <= nt - 1 if to_right else target >= 0
        starts = t == 0 if to_right else t == nt - 1
        further = target + 1 <= nt - 1 if to_right else target - 1 >= 0

        @pl.when(inside)
        def _():
            if d < nt - 1:
                @pl.when(starts)
                def _():
                    part(target, h, buf_s.at[d - 1, h], None)
                    link(d, h).wait_send()

                @pl.when(jnp.logical_not(starts))
                def _():
                    link(d, h).wait_recv()
                    part(target, h, buf_s.at[d - 1, h], buf_r.at[d, h])
                    if d < nt - 2:
                        @pl.when(further)
                        def _():
                            link(d, h).wait_send()
            else:
                part(target, h, buf_s.at[d - 1, h], None)
            link(d - 1, h).start()

    def chain_end(h, to_right):
        buf_s, buf_r, link = linker(to_right)
        at = pl.ds(h * part_rows, part_rows)

        @pl.when(t > 0 if to_right else t < nt - 1)
        def _():
            link(0, h).wait_recv()
            total[at, :] += buf_r[0, h].astype(F32)

        @pl.when(t < nt - 1 if to_right else t > 0)
        def _():
            link(0, h).wait_send()

    for d in range(nt - 1, 0, -1):
        for h in range(HALVES):
            chain(d, h, True)
            chain(d, h, False)
    for h in range(HALVES):
        part(t, h, total.at[pl.ds(h * part_rows, part_rows), :], None)
    inner_all = sum_tp(inn, inn_copies)
    inner_col = jnp.broadcast_to(inner_all[0:1], (128, rows)).T[:, :1]
    for h in range(HALVES):
        chain_end(h, True)
        chain_end(h, False)
    inverse = inv_ref[:, :1]
    mixed = inner_col / (inverse * width)
    factor = inverse * inverse * inverse * mixed

    def finish(j, carry):
        at = pl.ds(pl.multiple_of(j * block, block), block)
        far = pl.ds(pl.multiple_of(t * columns + j * block, block), block)
        scaled = total[:, at] * gain[:, far]
        grad_out[:, at] = (inverse * scaled - hidden[:, far].astype(F32) * factor).astype(BF16)
        return carry

    lax.fori_loop(0, columns // block, finish, 0)
    for copy in pending:
        copy.wait_send()


def local(
    hidden,
    norm_gain,
    gen_value,
    gen_head,
    critic_embed,
    critic_gain,
    critic_value,
    critic_head,
    noise,
    owner,
    tsteps,
    noise_mix,
    gap_weight,
):
    rows, width = hidden.shape
    depth, heads = gen_value.shape
    crit_rows, latent_width = noise.shape
    crit_cols = critic_value.shape[1]
    ns = lax.axis_size("seq")
    ng = lax.axis_size("group")
    nt = lax.axis_size("tp")
    group_id = lax.axis_index("group")
    seq_id = lax.axis_index("seq")
    if depth % 128 == 0:
        scaling = critic_gain
    else:
        critic_id = group_id // (ng // 2)
        first = seq_id * depth
        embed = lax.dynamic_slice(critic_embed, (critic_id, 0, first), (1, latent_width, depth))[0]
        gains = lax.dynamic_slice(critic_gain, (critic_id, first), (1, depth))
        scaling = jnp.concatenate(split_bf16(embed.astype(F32) * gains.astype(F32)), axis=0)

    shared = ng == 4 and depth % (128 * ng) == 0
    pieces = 8 if shared else 1
    vmem = pl.BlockSpec(memory_space=pltpu.VMEM)
    columns = width // nt
    dma = pltpu.SemaphoreType.DMA
    latent, grad = pl.pallas_call(
        functools.partial(kernel, ng, ns, nt, shared, pieces),
        out_shape=(
            jax.ShapeDtypeStruct((latent_width, rows), BF16),
            jax.ShapeDtypeStruct((rows, columns), BF16),
        ),
        in_specs=[vmem, vmem, pl.BlockSpec(memory_space=pl.ANY)] + [vmem] * 7
        + [pl.BlockSpec(memory_space=pltpu.SMEM), vmem, vmem],
        out_specs=(vmem, vmem),
        scratch_shapes=[
            pltpu.VMEM((1, width), F32),
            pltpu.VMEM((width, heads), BF16),
            pltpu.VMEM((rows, width), BF16),
            pltpu.VMEM((rows, 128), F32),
            pltpu.VMEM((rows, heads), F32),
            pltpu.VMEM((rows, heads), F32),
            pltpu.VMEM((ns, latent_width, crit_cols), F32),
            pltpu.VMEM((ng, crit_cols, 2 * latent_width), BF16),
            pltpu.VMEM((ng, latent_width, crit_cols), BF16),
            pltpu.VMEM((ns, latent_width, crit_rows), BF16),
            pltpu.VMEM((nt, latent_width, rows), BF16),
            pltpu.VMEM((nt, latent_width, rows), BF16),
            pltpu.VMEM((nt, 8, rows), F32),
            pltpu.VMEM((nt - 1, HALVES, rows // HALVES, columns), BF16),
            pltpu.VMEM((nt - 1, HALVES, rows // HALVES, columns), BF16),
            pltpu.VMEM((nt - 1, HALVES, rows // HALVES, columns), BF16),
            pltpu.VMEM((nt - 1, HALVES, rows // HALVES, columns), BF16),
            pltpu.VMEM((rows, columns), F32),
            dma,
            dma((ns - 1, pieces)),
            dma((ns - 1, pieces)),
            dma((3, ns - 1, pieces)),
            dma((3, ns - 1, pieces)),
            dma((ns - 1,)),
            dma((ns - 1,)),
            dma((ns - 1,)),
            dma((ns - 1,)),
            dma((ng - 1,)),
            dma((ng - 1,)),
            dma((ng - 1,)),
            dma((ng - 1,)),
            dma((3, nt - 1)),
            dma((3, nt - 1)),
            dma((nt - 1, HALVES)),
            dma((nt - 1, HALVES)),
            dma((nt - 1, HALVES)),
            dma((nt - 1, HALVES)),
        ],
        compiler_params=pltpu.CompilerParams(
            collective_id=0, has_side_effects=True, vmem_limit_bytes=56 * 1024 * 1024
        ),
    )(
        hidden, norm_gain, gen_value, gen_head.T, critic_embed, scaling, critic_value.T, critic_head.T,
        noise.T, owner, tsteps, noise_mix, gap_weight,
    )
    return latent.T, grad


def solution(mesh):
    return jax.shard_map(
        local,
        mesh=mesh,
        in_specs=(
            P(("group", "seq"), None),
            P(),
            P("seq", "tp"),
            P("tp", None),
            P(),
            P(),
            P("seq", ("group", "tp")),
            P(("group", "tp"), None),
            P("seq", None),
            P(("group", "seq")),
            P(),
            P(),
            P(),
        ),
        out_specs=(P(("group", "seq"), None), P(("group", "seq"), "tp")),
        check_vma=False,
    )
```

```python
import functools
import jax
import jax.numpy as jnp
from jax import lax
from jax.experimental import pallas as pl
from jax.experimental.pallas import tpu as pltpu
from jax.sharding import PartitionSpec as P

FTOK = 2048
HALVES = 2
MESH = pl.DeviceIdType.MESH
F32 = jnp.float32
BF16 = jnp.bfloat16
ROOT = 0.7978845608028654
CUBE = 0.044715


def split_bf16(v):
    hi = lax.reduce_precision(v, 8, 7)
    return hi.astype(BF16), (v - hi).astype(BF16)


def gelu_tanh(v):
    return 0.5 * v * (1.0 + jnp.tanh(ROOT * (v + CUBE * v * v * v)))


def dot(a, b):
    return jnp.dot(a, b, preferred_element_type=F32)


def dot_t(a, b):
    return lax.dot_general(a, b, (((1,), (1,)), ((), ())), preferred_element_type=F32)


def kernel(
    ng, ns, nt, shared, pieces,
    hidden_in, gain_in, weights, gen_head, embed_in, scaling, crit_value_in, crit_head, noise, owner, tsteps, tables, weighting,
    latent_out, grad_out,
    hidden, embed, crit_value, load_sem, gain, wall, normed, inv_ref, values, slope, mpart, mall, hall, noise_all, latp, gapp, inn,
    send_r, send_l, recv_r, recv_l, total,
    own_sem, w_send, w_recv, f_send, f_recv, m_send, m_recv, n_send, n_recv,
    g_send, g_recv, h_send, h_recv, t_send, t_recv, rs_sem, rr_sem, ls_sem, lr_sem,
):
    g = lax.axis_index("group")
    s = lax.axis_index("seq")
    t = lax.axis_index("tp")
    rows, width = hidden_in.shape
    depth = weights.shape[0]
    crit_rows = noise.shape[1]
    half = channels = noise.shape[0]
    columns = width // nt
    pending = []

    def seq_peer(o):
        return lax.rem(s + o, ns)

    def group_peer(o):
        return lax.rem(g + o, ng)

    def tp_peer(o):
        return lax.rem(t + o, nt)

    def push(src, dst, send, recv, where):
        copy = pltpu.make_async_remote_copy(
            src_ref=src, dst_ref=dst, send_sem=send, recv_sem=recv,
            device_id=where, device_id_type=MESH,
        )
        copy.start()
        pending.append(copy)
        return copy

    loads = []
    for k, (src, dst) in enumerate(((hidden_in, hidden), (crit_value_in, crit_value), (embed_in, embed))):
        loads.append(pltpu.make_async_copy(src, dst, load_sem.at[k]))
        loads[-1].start()

    barrier = pltpu.get_barrier_semaphore()
    for o in range(1, ns):
        pl.semaphore_signal(barrier, inc=1, device_id={"seq": seq_peer(o)}, device_id_type=MESH)
    for o in range(1, ng):
        pl.semaphore_signal(barrier, inc=1, device_id={"group": group_peer(o)}, device_id_type=MESH)
    for o in range(1, nt):
        pl.semaphore_signal(barrier, inc=1, device_id={"tp": tp_peer(o)}, device_id_type=MESH)
    pl.semaphore_wait(barrier, ns + ng + nt - 3)

    local = pltpu.make_async_copy(weights, wall.at[pl.ds(s * depth, depth), :], own_sem)
    local.start()
    quarter = depth // ng if shared else depth
    step = quarter // pieces
    mine = g * quarter if shared else 0
    w_copies = {}
    for p in range(pieces):
        for o in range(1, ns):
            w_copies[o, p] = push(
                weights.at[pl.ds(mine + p * step, step), :],
                wall.at[pl.ds(s * depth + mine + p * step, step), :],
                w_send.at[o - 1, p], w_recv.at[o - 1, p], {"seq": seq_peer(o)},
            )
    h_copies = [
        push(crit_head, hall.at[g], h_send.at[o - 1], h_recv.at[o - 1], {"group": group_peer(o)})
        for o in range(1, ng)
    ]
    noise_all[s] = noise[...]
    hall[g] = crit_head[...]

    def fold():
        if depth % 128 == 0:
            critic = g // (ng // 2)
            at = pl.ds(pl.multiple_of(s * depth, 128), depth)
            both = scaling[:, at].astype(F32)
            eg = embed[critic, :, at].astype(F32) * jnp.where(critic == 0, both[0:1], both[1:2])
            eg_high = eg.astype(BF16)
            eg_low = (eg - eg_high.astype(F32)).astype(BF16)
            eg_pair = jnp.concatenate([eg_high, eg_low], axis=0)
        else:
            eg_pair = scaling[...]
        folded = dot_t(eg_pair, crit_value[...])
        mpart[s] = folded[:half] + folded[half:]

    def norm_all():
        gain[...] = gain_in[...].astype(F32).reshape(1, width)

        def norm_rows(r, carry):
            at = pl.ds(pl.multiple_of(r * 32, 32), 32)
            x = hidden[at, :].astype(F32)
            inverse = lax.rsqrt(jnp.mean(x * x, axis=-1, keepdims=True) + 1e-06)
            normed[at, :] = (x * inverse * gain[...]).astype(BF16)
            inv_ref[at, :] = jnp.broadcast_to(inverse, (32, 128))
            return carry

        lax.fori_loop(0, rows // 32, norm_rows, 0)
        values[...] = jnp.zeros_like(values)

    def add_rows(start, size):
        at = pl.multiple_of(start, 128)
        values[...] += dot(normed[:, pl.ds(at, size)], wall[pl.ds(at, size), :])

    def own_rows(j, carry):
        add_rows(s * depth + j * quarter, quarter)
        return carry

    x_copies, c_copies, d_copies = {}, {}, {}

    def forward(p):
        for o in range(1, ns):
            w_copies[o, p].wait_recv()
            base = lax.rem(s - o + ns, ns) * depth
            at = pl.ds(base + mine + p * step, step)
            x_copies[o, p] = push(
                wall.at[at, :], wall.at[at, :],
                f_send.at[0, o - 1, p], f_recv.at[0, o - 1, p], {"group": g ^ 2},
            )
            c_copies[o, p] = push(
                wall.at[at, :], wall.at[at, :],
                f_send.at[1, o - 1, p], f_recv.at[1, o - 1, p], {"group": g ^ 1},
            )

    if shared:
        forward(0)
    loads[0].wait()
    norm_all()
    if shared:
        forward(1)
        forward(2)
    local.wait()
    if shared:
        lax.fori_loop(0, ng, own_rows, 0)
        forward(3)
    loads[1].wait()
    loads[2].wait()
    fold()
    if shared:
        for p in range(4, pieces):
            forward(p)
    n_copies = [
        push(noise, noise_all.at[s], n_send.at[o - 1], n_recv.at[o - 1], {"seq": seq_peer(o)})
        for o in range(1, ns)
    ]
    m_copies = [
        push(mpart.at[s], mpart.at[s], m_send.at[o - 1], m_recv.at[o - 1], {"seq": seq_peer(o)})
        for o in range(1, ns)
    ]
    if shared:
        for p in range(pieces):
            for o in range(1, ns):
                x_copies[o, p].wait_recv()
                base = lax.rem(s - o + ns, ns) * depth
                at = pl.ds(base + (g ^ 2) * quarter + p * step, step)
                d_copies[o, p] = push(
                    wall.at[at, :], wall.at[at, :],
                    f_send.at[2, o - 1, p], f_recv.at[2, o - 1, p], {"group": g ^ 1},
                )

    for copy in m_copies:
        copy.wait_recv()
    whole = mpart[0]
    for k in range(1, ns):
        whole = whole + mpart[k]
    high = whole.astype(BF16)
    high32 = high.astype(F32)
    cols = whole.shape[1]
    fill = -cols % 128
    both = jnp.concatenate([high32, whole - high32], axis=0)
    if fill:
        both = jnp.concatenate([both, jnp.zeros((2 * half, fill), F32)], axis=1)
    mall[g] = both.T[:cols].astype(BF16)
    g_copies = [
        push(mall.at[g], mall.at[g], g_send.at[o - 1], g_recv.at[o - 1], {"group": group_peer(o)})
        for o in range(1, ng)
    ]
    grams = []
    for which in range(2):
        gram = dot_t(embed[which], embed[which])
        first = gram.astype(BF16)
        rest = gram - first.astype(F32)
        second = rest.astype(BF16)
        grams.append((first, second, (rest - second.astype(F32)).astype(BF16)))
    for copy in n_copies:
        copy.wait_recv()

    def pick(k, carry):
        place = lax.broadcasted_iota(jnp.int32, (crit_rows, rows), 0) + k * crit_rows
        hot = jnp.where(place == owner_row, 1.0, 0.0).astype(BF16)
        return carry + dot(noise_all[k], hot)

    owner_row = owner[...].reshape(1, rows)
    noise_rows = lax.fori_loop(0, ns, pick, jnp.zeros((channels, rows), F32))
    level = tsteps[((g * ns + s) * rows) // FTOK]
    levels = tables.shape[1]
    found = lax.broadcasted_iota(jnp.int32, (1, levels), 1) == level
    mix = jnp.sum(jnp.where(found, tables[...], 0.0), axis=1, keepdims=True)
    weight = jnp.sum(jnp.where(found, weighting[...].reshape(1, levels), 0.0), axis=1, keepdims=True)

    if shared:
        for o in range(1, ns):
            base = lax.rem(s - o + ns, ns) * depth
            add_rows(base + g * quarter, quarter)
            add_rows(base + (g ^ 2) * quarter, quarter)
            for p in range(pieces):
                c_copies[o, p].wait_recv()
            add_rows(base + (g ^ 1) * quarter, quarter)
            for p in range(pieces):
                d_copies[o, p].wait_recv()
            add_rows(base + (g ^ 3) * quarter, quarter)
    else:
        for copy in w_copies.values():
            copy.wait_recv()

        def all_rows(j, carry):
            add_rows(j * (width // 8), width // 8)
            return carry

        lax.fori_loop(0, 8, all_rows, 0)

    def share_tp(buffer, index):
        return [
            push(buffer.at[t], buffer.at[t], t_send.at[index, o - 1], t_recv.at[index, o - 1], {"tp": tp_peer(o)})
            for o in range(1, nt)
        ]

    def sum_tp(buffer, copies):
        for copy in copies:
            copy.wait_recv()
        out = buffer[0].astype(F32)
        for k in range(1, nt):
            out = out + buffer[k].astype(F32)
        return out

    v = values[...]
    tanh = jnp.tanh(ROOT * (v + CUBE * v * v * v))
    latp[t] = dot_t(gen_head[...], (0.5 * v * (1.0 + tanh)).astype(BF16)).astype(BF16)
    lat_copies = share_tp(latp, 0)
    slope[...] = 0.5 * (1.0 + tanh) + 0.5 * v * (1.0 - tanh * tanh) * ROOT * (1.0 + 3.0 * CUBE * v * v)
    for copy in g_copies + h_copies:
        copy.wait_recv()
    latent = sum_tp(latp, lat_copies).astype(BF16)
    latent_out[...] = latent

    noisy = (mix[0:1] * latent.astype(F32) + mix[1:2] * noise_rows).astype(BF16)
    noisy32 = noisy.astype(F32)
    scales = []
    for which in range(2):
        a, b, c = grams[which]
        quad = jnp.sum((dot(a, noisy) + dot(b, noisy) + dot(c, noisy)) * noisy32, axis=0, keepdims=True)
        scales.append(lax.rsqrt(jnp.maximum(quad, 0.0) / width + 1e-06))
    pair = jnp.concatenate([noisy, noisy], axis=0)
    gap = jnp.zeros((channels, rows), F32)
    for member in range(ng):
        which = member // (ng // 2)
        act = gelu_tanh(dot(mall[member], pair) * scales[which]).astype(BF16)
        term = dot(hall[member], act)
        gap = gap + term if which else gap - term
    gapp[t] = gap.astype(BF16)
    gap = sum_tp(gapp, share_tp(gapp, 1))
    pull = weight * gap
    fill = -channels % 128
    if fill:
        pull = jnp.concatenate([pull, jnp.zeros((fill, rows), F32)], axis=0)
    cotangent = pull.T[:, :channels].astype(BF16)

    grad_values = (slope[...] * dot(cotangent, gen_head[...])).astype(BF16)
    inner = jnp.sum(grad_values.astype(F32) * values[...], axis=-1, keepdims=True)
    inn[t] = jnp.broadcast_to(inner, (rows, 128)).T[:8]
    inn_copies = share_tp(inn, 2)

    block = 256 if columns % 256 == 0 else columns
    part_rows = rows // HALVES

    def part(q, h, out, extra):
        lhs = grad_values[h * part_rows:(h + 1) * part_rows]

        def one(j, carry):
            at = pl.ds(pl.multiple_of(j * block, block), block)
            w = wall[pl.ds(pl.multiple_of(q * columns + j * block, block), block), :]
            term = dot_t(lhs, w)
            if extra is not None:
                term = term + extra[:, at].astype(F32)
            out[:, at] = term.astype(out.dtype)
            return carry

        lax.fori_loop(0, columns // block, one, 0)

    def linker(to_right):
        buf_s, buf_r = (send_r, recv_r) if to_right else (send_l, recv_l)
        sem_s, sem_r = (rs_sem, rr_sem) if to_right else (ls_sem, lr_sem)

        def link(k, h):
            return pltpu.make_async_remote_copy(
                src_ref=buf_s.at[k, h], dst_ref=buf_r.at[k, h], send_sem=sem_s.at[k, h], recv_sem=sem_r.at[k, h],
                device_id={"tp": t + 1 if to_right else t - 1}, device_id_type=MESH,
            )

        return buf_s, buf_r, link

    def chain(d, h, to_right):
        buf_s, buf_r, link = linker(to_right)
        target = t + d if to_right else t - d
        inside = target <= nt - 1 if to_right else target >= 0
        starts = t == 0 if to_right else t == nt - 1
        further = target + 1 <= nt - 1 if to_right else target - 1 >= 0

        @pl.when(inside)
        def _():
            if d < nt - 1:
                @pl.when(starts)
                def _():
                    part(target, h, buf_s.at[d - 1, h], None)
                    link(d, h).wait_send()

                @pl.when(jnp.logical_not(starts))
                def _():
                    link(d, h).wait_recv()
                    part(target, h, buf_s.at[d - 1, h], buf_r.at[d, h])
                    if d < nt - 2:
                        @pl.when(further)
                        def _():
                            link(d, h).wait_send()
            else:
                part(target, h, buf_s.at[d - 1, h], None)
            link(d - 1, h).start()

    def chain_end(h, to_right):
        buf_s, buf_r, link = linker(to_right)
        at = pl.ds(h * part_rows, part_rows)

        @pl.when(t > 0 if to_right else t < nt - 1)
        def _():
            link(0, h).wait_recv()
            total[at, :] += buf_r[0, h].astype(F32)

        @pl.when(t < nt - 1 if to_right else t > 0)
        def _():
            link(0, h).wait_send()

    for d in range(nt - 1, 0, -1):
        for h in range(HALVES):
            chain(d, h, True)
            chain(d, h, False)
    for h in range(HALVES):
        part(t, h, total.at[pl.ds(h * part_rows, part_rows), :], None)
    inner_all = sum_tp(inn, inn_copies)
    inner_col = jnp.broadcast_to(inner_all[0:1], (128, rows)).T[:, :1]
    for h in range(HALVES):
        chain_end(h, True)
        chain_end(h, False)
    inverse = inv_ref[:, :1]
    mixed = inner_col / (inverse * width)
    factor = inverse * inverse * inverse * mixed

    def finish(j, carry):
        at = pl.ds(pl.multiple_of(j * block, block), block)
        far = pl.ds(pl.multiple_of(t * columns + j * block, block), block)
        scaled = total[:, at] * gain[:, far]
        grad_out[:, at] = (inverse * scaled - hidden[:, far].astype(F32) * factor).astype(BF16)
        return carry

    lax.fori_loop(0, columns // block, finish, 0)
    for copy in pending:
        copy.wait_send()


def local(
    hidden,
    norm_gain,
    gen_value,
    gen_head,
    critic_embed,
    critic_gain,
    critic_value,
    critic_head,
    noise,
    owner,
    tsteps,
    noise_mix,
    gap_weight,
):
    rows, width = hidden.shape
    depth, heads = gen_value.shape
    crit_rows, latent_width = noise.shape
    crit_cols = critic_value.shape[1]
    ns = lax.axis_size("seq")
    ng = lax.axis_size("group")
    nt = lax.axis_size("tp")
    group_id = lax.axis_index("group")
    seq_id = lax.axis_index("seq")
    if depth % 128 == 0:
        scaling = critic_gain
    else:
        critic_id = group_id // (ng // 2)
        first = seq_id * depth
        embed = lax.dynamic_slice(critic_embed, (critic_id, 0, first), (1, latent_width, depth))[0]
        gains = lax.dynamic_slice(critic_gain, (critic_id, first), (1, depth))
        scaling = jnp.concatenate(split_bf16(embed.astype(F32) * gains.astype(F32)), axis=0)

    shared = ng == 4 and depth % (128 * ng) == 0
    pieces = 8 if shared else 1
    vmem = pl.BlockSpec(memory_space=pltpu.VMEM)
    far = pl.BlockSpec(memory_space=pl.ANY)
    columns = width // nt
    dma = pltpu.SemaphoreType.DMA
    latent, grad = pl.pallas_call(
        functools.partial(kernel, ng, ns, nt, shared, pieces),
        out_shape=(
            jax.ShapeDtypeStruct((latent_width, rows), BF16),
            jax.ShapeDtypeStruct((rows, columns), BF16),
        ),
        in_specs=[far, vmem, far, vmem, far, vmem, far] + [vmem] * 3
        + [pl.BlockSpec(memory_space=pltpu.SMEM), vmem, vmem],
        out_specs=(vmem, vmem),
        scratch_shapes=[
            pltpu.VMEM((rows, width), BF16),
            pltpu.VMEM(critic_embed.shape, BF16),
            pltpu.VMEM((crit_cols, depth), BF16),
            dma((3,)),
            pltpu.VMEM((1, width), F32),
            pltpu.VMEM((width, heads), BF16),
            pltpu.VMEM((rows, width), BF16),
            pltpu.VMEM((rows, 128), F32),
            pltpu.VMEM((rows, heads), F32),
            pltpu.VMEM((rows, heads), F32),
            pltpu.VMEM((ns, latent_width, crit_cols), F32),
            pltpu.VMEM((ng, crit_cols, 2 * latent_width), BF16),
            pltpu.VMEM((ng, latent_width, crit_cols), BF16),
            pltpu.VMEM((ns, latent_width, crit_rows), BF16),
            pltpu.VMEM((nt, latent_width, rows), BF16),
            pltpu.VMEM((nt, latent_width, rows), BF16),
            pltpu.VMEM((nt, 8, rows), F32),
            pltpu.VMEM((nt - 1, HALVES, rows // HALVES, columns), BF16),
            pltpu.VMEM((nt - 1, HALVES, rows // HALVES, columns), BF16),
            pltpu.VMEM((nt - 1, HALVES, rows // HALVES, columns), BF16),
            pltpu.VMEM((nt - 1, HALVES, rows // HALVES, columns), BF16),
            pltpu.VMEM((rows, columns), F32),
            dma,
            dma((ns - 1, pieces)),
            dma((ns - 1, pieces)),
            dma((3, ns - 1, pieces)),
            dma((3, ns - 1, pieces)),
            dma((ns - 1,)),
            dma((ns - 1,)),
            dma((ns - 1,)),
            dma((ns - 1,)),
            dma((ng - 1,)),
            dma((ng - 1,)),
            dma((ng - 1,)),
            dma((ng - 1,)),
            dma((3, nt - 1)),
            dma((3, nt - 1)),
            dma((nt - 1, HALVES)),
            dma((nt - 1, HALVES)),
            dma((nt - 1, HALVES)),
            dma((nt - 1, HALVES)),
        ],
        compiler_params=pltpu.CompilerParams(
            collective_id=0, has_side_effects=True, vmem_limit_bytes=56 * 1024 * 1024
        ),
    )(
        hidden, norm_gain, gen_value, gen_head.T, critic_embed, scaling, critic_value.T, critic_head.T,
        noise.T, owner, tsteps, noise_mix, gap_weight,
    )
    return latent.T, grad


def solution(mesh):
    return jax.shard_map(
        local,
        mesh=mesh,
        in_specs=(
            P(("group", "seq"), None),
            P(),
            P("seq", "tp"),
            P("tp", None),
            P(),
            P(),
            P("seq", ("group", "tp")),
            P(("group", "tp"), None),
            P("seq", None),
            P(("group", "seq")),
            P(),
            P(),
            P(),
        ),
        out_specs=(P(("group", "seq"), None), P(("group", "seq"), "tp")),
        check_vma=False,
    )
```

```python
import functools
import jax
import jax.numpy as jnp
from jax import lax
from jax.experimental import pallas as pl
from jax.experimental.pallas import tpu as pltpu
from jax.sharding import PartitionSpec as P

FTOK = 2048
HALVES = 2
MESH = pl.DeviceIdType.MESH
F32 = jnp.float32
BF16 = jnp.bfloat16
ROOT = 0.7978845608028654
CUBE = 0.044715


def split_bf16(v):
    hi = lax.reduce_precision(v, 8, 7)
    return hi.astype(BF16), (v - hi).astype(BF16)


def gelu_tanh(v):
    return 0.5 * v * (1.0 + jnp.tanh(ROOT * (v + CUBE * v * v * v)))


def dot(a, b):
    return jnp.dot(a, b, preferred_element_type=F32)


def dot_t(a, b):
    return lax.dot_general(a, b, (((1,), (1,)), ((), ())), preferred_element_type=F32)


def kernel(
    ng, ns, nt, shared, pieces,
    hidden_in, gain_in, weights, gen_head, embed_in, scaling, crit_value_in, crit_head, noise, owner, tsteps, tables, weighting,
    latent_out, grad_out,
    hidden, embed, crit_value, load_sem, gain, wall, normed, inv_ref, values, slope, mpart, mall, hall, noise_all, latp, gapp, inn,
    send_r, send_l, recv_r, recv_l, total,
    wextra, gv_ref, gv_far, z_send, z_recv, zc_sem, gv_sem,
    own_sem, w_send, w_recv, f_send, f_recv, m_send, m_recv, n_send, n_recv,
    g_send, g_recv, h_send, h_recv, t_send, t_recv, rs_sem, rr_sem, ls_sem, lr_sem,
):
    g = lax.axis_index("group")
    s = lax.axis_index("seq")
    t = lax.axis_index("tp")
    rows, width = hidden_in.shape
    depth = weights.shape[0]
    crit_rows = noise.shape[1]
    half = channels = noise.shape[0]
    columns = width // nt
    pending = []

    def seq_peer(o):
        return lax.rem(s + o, ns)

    def group_peer(o):
        return lax.rem(g + o, ng)

    def tp_peer(o):
        return lax.rem(t + o, nt)

    def push(src, dst, send, recv, where):
        copy = pltpu.make_async_remote_copy(
            src_ref=src, dst_ref=dst, send_sem=send, recv_sem=recv,
            device_id=where, device_id_type=MESH,
        )
        copy.start()
        pending.append(copy)
        return copy

    loads = []
    for k, (src, dst) in enumerate(((hidden_in, hidden), (crit_value_in, crit_value), (embed_in, embed))):
        loads.append(pltpu.make_async_copy(src, dst, load_sem.at[k]))
        loads[-1].start()

    barrier = pltpu.get_barrier_semaphore()
    for o in range(1, ns):
        pl.semaphore_signal(barrier, inc=1, device_id={"seq": seq_peer(o)}, device_id_type=MESH)
    for o in range(1, ng):
        pl.semaphore_signal(barrier, inc=1, device_id={"group": group_peer(o)}, device_id_type=MESH)
    for o in range(1, nt):
        pl.semaphore_signal(barrier, inc=1, device_id={"tp": tp_peer(o)}, device_id_type=MESH)
    pl.semaphore_wait(barrier, ns + ng + nt - 3)

    local = pltpu.make_async_copy(weights, wall.at[pl.ds(s * depth, depth), :], own_sem)
    local.start()
    quarter = depth // ng if shared else depth
    step = quarter // pieces
    mine = g * quarter if shared else 0
    near = shared and nt == 4 and ns == 2 and 2 * quarter == columns
    edge = jnp.logical_or(t == 0, t == nt - 1)
    middle = jnp.logical_not(edge)
    inward = {"tp": jnp.where(t == 0, 1, nt - 2)}
    odd = lax.rem(g, 2)
    want_half = jnp.where(t == 0, 0, 1)
    want_quarter = jnp.where(t == 0, 2, 0) + odd

    def hand(src, p):
        return pltpu.make_async_remote_copy(
            src_ref=src, dst_ref=wextra.at[pl.ds(odd * quarter + p * step, step), :],
            send_sem=z_send.at[p], recv_sem=z_recv.at[p], device_id=inward, device_id_type=MESH,
        )

    def hand_far(p, index):
        @pl.when(jnp.logical_and(edge, jnp.logical_and(s != want_half, want_quarter == index)))
        def _():
            hand(wall.at[pl.ds((1 - s) * depth + index * quarter + p * step, step), :], p).start()

    w_copies = {}
    for p in range(pieces):
        for o in range(1, ns):
            w_copies[o, p] = push(
                weights.at[pl.ds(mine + p * step, step), :],
                wall.at[pl.ds(s * depth + mine + p * step, step), :],
                w_send.at[o - 1, p], w_recv.at[o - 1, p], {"seq": seq_peer(o)},
            )
    if near:
        @pl.when(jnp.logical_and(edge, s == want_half))
        def _():
            for p in range(pieces):
                hand(weights.at[pl.ds(want_quarter * quarter + p * step, step), :], p).start()

    h_copies = [
        push(crit_head, hall.at[g], h_send.at[o - 1], h_recv.at[o - 1], {"group": group_peer(o)})
        for o in range(1, ng)
    ]
    noise_all[s] = noise[...]
    hall[g] = crit_head[...]

    def fold():
        if depth % 128 == 0:
            critic = g // (ng // 2)
            at = pl.ds(pl.multiple_of(s * depth, 128), depth)
            both = scaling[:, at].astype(F32)
            eg = embed[critic, :, at].astype(F32) * jnp.where(critic == 0, both[0:1], both[1:2])
            eg_high = eg.astype(BF16)
            eg_low = (eg - eg_high.astype(F32)).astype(BF16)
            eg_pair = jnp.concatenate([eg_high, eg_low], axis=0)
        else:
            eg_pair = scaling[...]
        folded = dot_t(eg_pair, crit_value[...])
        mpart[s] = folded[:half] + folded[half:]

    def norm_all():
        gain[...] = gain_in[...].astype(F32).reshape(1, width)

        def norm_rows(r, carry):
            at = pl.ds(pl.multiple_of(r * 32, 32), 32)
            x = hidden[at, :].astype(F32)
            inverse = lax.rsqrt(jnp.mean(x * x, axis=-1, keepdims=True) + 1e-06)
            normed[at, :] = (x * inverse * gain[...]).astype(BF16)
            inv_ref[at, :] = jnp.broadcast_to(inverse, (32, 128))
            return carry

        lax.fori_loop(0, rows // 32, norm_rows, 0)
        values[...] = jnp.zeros_like(values)

    def add_rows(start, size):
        at = pl.multiple_of(start, 128)
        values[...] += dot(normed[:, pl.ds(at, size)], wall[pl.ds(at, size), :])

    def own_rows(j, carry):
        add_rows(s * depth + j * quarter, quarter)
        return carry

    x_copies, c_copies, d_copies = {}, {}, {}

    def forward(p):
        for o in range(1, ns):
            w_copies[o, p].wait_recv()
            base = lax.rem(s - o + ns, ns) * depth
            at = pl.ds(base + mine + p * step, step)
            x_copies[o, p] = push(
                wall.at[at, :], wall.at[at, :],
                f_send.at[0, o - 1, p], f_recv.at[0, o - 1, p], {"group": g ^ 2},
            )
            c_copies[o, p] = push(
                wall.at[at, :], wall.at[at, :],
                f_send.at[1, o - 1, p], f_recv.at[1, o - 1, p], {"group": g ^ 1},
            )
        if near:
            hand_far(p, g)

    if shared:
        forward(0)
    loads[0].wait()
    norm_all()
    if shared:
        forward(1)
        forward(2)
    local.wait()
    if shared:
        lax.fori_loop(0, ng, own_rows, 0)
        forward(3)
    loads[1].wait()
    loads[2].wait()
    fold()
    if shared:
        for p in range(4, pieces):
            forward(p)
    n_copies = [
        push(noise, noise_all.at[s], n_send.at[o - 1], n_recv.at[o - 1], {"seq": seq_peer(o)})
        for o in range(1, ns)
    ]
    m_copies = [
        push(mpart.at[s], mpart.at[s], m_send.at[o - 1], m_recv.at[o - 1], {"seq": seq_peer(o)})
        for o in range(1, ns)
    ]
    if shared:
        for p in range(pieces):
            for o in range(1, ns):
                x_copies[o, p].wait_recv()
                base = lax.rem(s - o + ns, ns) * depth
                at = pl.ds(base + (g ^ 2) * quarter + p * step, step)
                d_copies[o, p] = push(
                    wall.at[at, :], wall.at[at, :],
                    f_send.at[2, o - 1, p], f_recv.at[2, o - 1, p], {"group": g ^ 1},
                )
            if near:
                hand_far(p, g ^ 2)

    for copy in m_copies:
        copy.wait_recv()
    whole = mpart[0]
    for k in range(1, ns):
        whole = whole + mpart[k]
    high = whole.astype(BF16)
    high32 = high.astype(F32)
    cols = whole.shape[1]
    fill = -cols % 128
    both = jnp.concatenate([high32, whole - high32], axis=0)
    if fill:
        both = jnp.concatenate([both, jnp.zeros((2 * half, fill), F32)], axis=1)
    mall[g] = both.T[:cols].astype(BF16)
    g_copies = [
        push(mall.at[g], mall.at[g], g_send.at[o - 1], g_recv.at[o - 1], {"group": group_peer(o)})
        for o in range(1, ng)
    ]
    grams = []
    for which in range(2):
        gram = dot_t(embed[which], embed[which])
        first = gram.astype(BF16)
        rest = gram - first.astype(F32)
        second = rest.astype(BF16)
        grams.append((first, second, (rest - second.astype(F32)).astype(BF16)))
    for copy in n_copies:
        copy.wait_recv()

    def pick(k, carry):
        place = lax.broadcasted_iota(jnp.int32, (crit_rows, rows), 0) + k * crit_rows
        hot = jnp.where(place == owner_row, 1.0, 0.0).astype(BF16)
        return carry + dot(noise_all[k], hot)

    owner_row = owner[...].reshape(1, rows)
    noise_rows = lax.fori_loop(0, ns, pick, jnp.zeros((channels, rows), F32))
    level = tsteps[((g * ns + s) * rows) // FTOK]
    levels = tables.shape[1]
    found = lax.broadcasted_iota(jnp.int32, (1, levels), 1) == level
    mix = jnp.sum(jnp.where(found, tables[...], 0.0), axis=1, keepdims=True)
    weight = jnp.sum(jnp.where(found, weighting[...].reshape(1, levels), 0.0), axis=1, keepdims=True)

    if shared:
        for o in range(1, ns):
            base = lax.rem(s - o + ns, ns) * depth
            add_rows(base + g * quarter, quarter)
            add_rows(base + (g ^ 2) * quarter, quarter)
            for p in range(pieces):
                c_copies[o, p].wait_recv()
            add_rows(base + (g ^ 1) * quarter, quarter)
            for p in range(pieces):
                d_copies[o, p].wait_recv()
            add_rows(base + (g ^ 3) * quarter, quarter)
    else:
        for copy in w_copies.values():
            copy.wait_recv()

        def all_rows(j, carry):
            add_rows(j * (width // 8), width // 8)
            return carry

        lax.fori_loop(0, 8, all_rows, 0)

    def share_tp(buffer, index):
        return [
            push(buffer.at[t], buffer.at[t], t_send.at[index, o - 1], t_recv.at[index, o - 1], {"tp": tp_peer(o)})
            for o in range(1, nt)
        ]

    def sum_tp(buffer, copies):
        for copy in copies:
            copy.wait_recv()
        out = buffer[0].astype(F32)
        for k in range(1, nt):
            out = out + buffer[k].astype(F32)
        return out

    v = values[...]
    tanh = jnp.tanh(ROOT * (v + CUBE * v * v * v))
    latp[t] = dot_t(gen_head[...], (0.5 * v * (1.0 + tanh)).astype(BF16)).astype(BF16)
    lat_copies = share_tp(latp, 0)
    slope[...] = 0.5 * (1.0 + tanh) + 0.5 * v * (1.0 - tanh * tanh) * ROOT * (1.0 + 3.0 * CUBE * v * v)
    for copy in g_copies + h_copies:
        copy.wait_recv()
    latent = sum_tp(latp, lat_copies).astype(BF16)
    latent_out[...] = latent

    noisy = (mix[0:1] * latent.astype(F32) + mix[1:2] * noise_rows).astype(BF16)
    noisy32 = noisy.astype(F32)
    scales = []
    for which in range(2):
        a, b, c = grams[which]
        quad = jnp.sum((dot(a, noisy) + dot(b, noisy) + dot(c, noisy)) * noisy32, axis=0, keepdims=True)
        scales.append(lax.rsqrt(jnp.maximum(quad, 0.0) / width + 1e-06))
    pair = jnp.concatenate([noisy, noisy], axis=0)
    gap = jnp.zeros((channels, rows), F32)
    for member in range(ng):
        which = member // (ng // 2)
        act = gelu_tanh(dot(mall[member], pair) * scales[which]).astype(BF16)
        term = dot(hall[member], act)
        gap = gap + term if which else gap - term
    gapp[t] = gap.astype(BF16)
    gap = sum_tp(gapp, share_tp(gapp, 1))
    pull = weight * gap
    fill = -channels % 128
    if fill:
        pull = jnp.concatenate([pull, jnp.zeros((fill, rows), F32)], axis=0)
    cotangent = pull.T[:, :channels].astype(BF16)

    grad_values = (slope[...] * dot(cotangent, gen_head[...])).astype(BF16)
    inner = jnp.sum(grad_values.astype(F32) * values[...], axis=-1, keepdims=True)
    inn[t] = jnp.broadcast_to(inner, (rows, 128)).T[:8]
    inn_copies = share_tp(inn, 2)

    if near:
        gv_ref[...] = grad_values
    mate_rows = wextra.at[pl.ds(odd * quarter, quarter), :] if near else wextra
    mate = pltpu.make_async_remote_copy(
        src_ref=mate_rows, dst_ref=mate_rows, send_sem=zc_sem.at[0], recv_sem=zc_sem.at[1],
        device_id={"group": g ^ 1}, device_id_type=MESH,
    )
    give = pltpu.make_async_remote_copy(
        src_ref=gv_ref, dst_ref=gv_far, send_sem=gv_sem.at[0], recv_sem=gv_sem.at[1],
        device_id=inward, device_id_type=MESH,
    )
    if near:
        @pl.when(middle)
        def _():
            for p in range(pieces):
                hand(wextra.at[pl.ds(odd * quarter + p * step, step), :], p).wait_recv()
            mate.start()

    block = 256 if columns % 256 == 0 else columns
    part_rows = rows // HALVES

    def part(q, h, out, extra):
        lhs = grad_values[h * part_rows:(h + 1) * part_rows]

        def one(j, carry):
            at = pl.ds(pl.multiple_of(j * block, block), block)
            w = wall[pl.ds(pl.multiple_of(q * columns + j * block, block), block), :]
            term = dot_t(lhs, w)
            if extra is not None:
                term = term + extra[:, at].astype(F32)
            out[:, at] = term.astype(out.dtype)
            return carry

        lax.fori_loop(0, columns // block, one, 0)

    def linker(to_right):
        buf_s, buf_r = (send_r, recv_r) if to_right else (send_l, recv_l)
        sem_s, sem_r = (rs_sem, rr_sem) if to_right else (ls_sem, lr_sem)

        def link(k, h):
            return pltpu.make_async_remote_copy(
                src_ref=buf_s.at[k, h], dst_ref=buf_r.at[k, h], send_sem=sem_s.at[k, h], recv_sem=sem_r.at[k, h],
                device_id={"tp": t + 1 if to_right else t - 1}, device_id_type=MESH,
            )

        return buf_s, buf_r, link

    def chain(d, h, to_right):
        buf_s, buf_r, link = linker(to_right)
        target = t + d if to_right else t - d
        inside = target <= nt - 1 if to_right else target >= 0
        starts = t == 0 if to_right else t == nt - 1
        further = target + 1 <= nt - 1 if to_right else target - 1 >= 0

        @pl.when(inside)
        def _():
            if d < nt - 1:
                @pl.when(starts)
                def _():
                    if near and d == 1:
                        link(d, h).wait_send()
                        if h == HALVES - 1:
                            give.start()
                    else:
                        part(target, h, buf_s.at[d - 1, h], None)
                        link(d, h).wait_send()

                @pl.when(jnp.logical_not(starts))
                def _():
                    link(d, h).wait_recv()
                    part(target, h, buf_s.at[d - 1, h], buf_r.at[d, h])
                    if d < nt - 2:
                        @pl.when(further)
                        def _():
                            link(d, h).wait_send()
            else:
                part(target, h, buf_s.at[d - 1, h], None)
            if near and d == 1:
                @pl.when(jnp.logical_not(starts))
                def _():
                    link(d - 1, h).start()
            else:
                link(d - 1, h).start()

    def chain_end(h, to_right):
        buf_s, buf_r, link = linker(to_right)
        at = pl.ds(h * part_rows, part_rows)

        skip = 1 if near else 0

        @pl.when(t > skip if to_right else t < nt - 1 - skip)
        def _():
            link(0, h).wait_recv()
            total[at, :] += buf_r[0, h].astype(F32)

        @pl.when(middle if near else (t < nt - 1 if to_right else t > 0))
        def _():
            link(0, h).wait_send()

    for d in range(nt - 1, 0, -1):
        for h in range(HALVES):
            chain(d, h, True)
            chain(d, h, False)
    for h in range(HALVES):
        part(t, h, total.at[pl.ds(h * part_rows, part_rows), :], None)
    inner_all = sum_tp(inn, inn_copies)
    inner_col = jnp.broadcast_to(inner_all[0:1], (128, rows)).T[:, :1]
    for h in range(HALVES):
        chain_end(h, True)
        chain_end(h, False)
    if near:
        @pl.when(middle)
        def _():
            mate.wait_recv()
            give.wait_recv()

            def near_part(j, carry):
                at = pl.ds(pl.multiple_of(j * block, block), block)
                total[:, at] += dot_t(gv_far[...], wextra[at, :])
                return carry

            lax.fori_loop(0, columns // block, near_part, 0)
            mate.wait_send()

        @pl.when(edge)
        def _():
            give.wait_send()
            for p in range(pieces):
                hand(wextra.at[pl.ds(odd * quarter + p * step, step), :], p).wait_send()

    inverse = inv_ref[:, :1]
    mixed = inner_col / (inverse * width)
    factor = inverse * inverse * inverse * mixed

    def finish(j, carry):
        at = pl.ds(pl.multiple_of(j * block, block), block)
        far = pl.ds(pl.multiple_of(t * columns + j * block, block), block)
        scaled = total[:, at] * gain[:, far]
        grad_out[:, at] = (inverse * scaled - hidden[:, far].astype(F32) * factor).astype(BF16)
        return carry

    lax.fori_loop(0, columns // block, finish, 0)
    for copy in pending:
        copy.wait_send()


def local(
    hidden,
    norm_gain,
    gen_value,
    gen_head,
    critic_embed,
    critic_gain,
    critic_value,
    critic_head,
    noise,
    owner,
    tsteps,
    noise_mix,
    gap_weight,
):
    rows, width = hidden.shape
    depth, heads = gen_value.shape
    crit_rows, latent_width = noise.shape
    crit_cols = critic_value.shape[1]
    ns = lax.axis_size("seq")
    ng = lax.axis_size("group")
    nt = lax.axis_size("tp")
    group_id = lax.axis_index("group")
    seq_id = lax.axis_index("seq")
    if depth % 128 == 0:
        scaling = critic_gain
    else:
        critic_id = group_id // (ng // 2)
        first = seq_id * depth
        embed = lax.dynamic_slice(critic_embed, (critic_id, 0, first), (1, latent_width, depth))[0]
        gains = lax.dynamic_slice(critic_gain, (critic_id, first), (1, depth))
        scaling = jnp.concatenate(split_bf16(embed.astype(F32) * gains.astype(F32)), axis=0)

    shared = ng == 4 and depth % (128 * ng) == 0
    pieces = 8 if shared else 1
    vmem = pl.BlockSpec(memory_space=pltpu.VMEM)
    far = pl.BlockSpec(memory_space=pl.ANY)
    columns = width // nt
    dma = pltpu.SemaphoreType.DMA
    latent, grad = pl.pallas_call(
        functools.partial(kernel, ng, ns, nt, shared, pieces),
        out_shape=(
            jax.ShapeDtypeStruct((latent_width, rows), BF16),
            jax.ShapeDtypeStruct((rows, columns), BF16),
        ),
        in_specs=[far, vmem, far, vmem, far, vmem, far] + [vmem] * 3
        + [pl.BlockSpec(memory_space=pltpu.SMEM), vmem, vmem],
        out_specs=(vmem, vmem),
        scratch_shapes=[
            pltpu.VMEM((rows, width), BF16),
            pltpu.VMEM(critic_embed.shape, BF16),
            pltpu.VMEM((crit_cols, depth), BF16),
            dma((3,)),
            pltpu.VMEM((1, width), F32),
            pltpu.VMEM((width, heads), BF16),
            pltpu.VMEM((rows, width), BF16),
            pltpu.VMEM((rows, 128), F32),
            pltpu.VMEM((rows, heads), F32),
            pltpu.VMEM((rows, heads), F32),
            pltpu.VMEM((ns, latent_width, crit_cols), F32),
            pltpu.VMEM((ng, crit_cols, 2 * latent_width), BF16),
            pltpu.VMEM((ng, latent_width, crit_cols), BF16),
            pltpu.VMEM((ns, latent_width, crit_rows), BF16),
            pltpu.VMEM((nt, latent_width, rows), BF16),
            pltpu.VMEM((nt, latent_width, rows), BF16),
            pltpu.VMEM((nt, 8, rows), F32),
            pltpu.VMEM((nt - 1, HALVES, rows // HALVES, columns), BF16),
            pltpu.VMEM((nt - 1, HALVES, rows // HALVES, columns), BF16),
            pltpu.VMEM((nt - 1, HALVES, rows // HALVES, columns), BF16),
            pltpu.VMEM((nt - 1, HALVES, rows // HALVES, columns), BF16),
            pltpu.VMEM((rows, columns), F32),
            pltpu.VMEM((columns, heads), BF16),
            pltpu.VMEM((rows, heads), BF16),
            pltpu.VMEM((rows, heads), BF16),
            dma((pieces,)),
            dma((pieces,)),
            dma((2,)),
            dma((2,)),
            dma,
            dma((ns - 1, pieces)),
            dma((ns - 1, pieces)),
            dma((3, ns - 1, pieces)),
            dma((3, ns - 1, pieces)),
            dma((ns - 1,)),
            dma((ns - 1,)),
            dma((ns - 1,)),
            dma((ns - 1,)),
            dma((ng - 1,)),
            dma((ng - 1,)),
            dma((ng - 1,)),
            dma((ng - 1,)),
            dma((3, nt - 1)),
            dma((3, nt - 1)),
            dma((nt - 1, HALVES)),
            dma((nt - 1, HALVES)),
            dma((nt - 1, HALVES)),
            dma((nt - 1, HALVES)),
        ],
        compiler_params=pltpu.CompilerParams(
            collective_id=0, has_side_effects=True, vmem_limit_bytes=56 * 1024 * 1024
        ),
    )(
        hidden, norm_gain, gen_value, gen_head.T, critic_embed, scaling, critic_value.T, critic_head.T,
        noise.T, owner, tsteps, noise_mix, gap_weight,
    )
    return latent.T, grad


def solution(mesh):
    return jax.shard_map(
        local,
        mesh=mesh,
        in_specs=(
            P(("group", "seq"), None),
            P(),
            P("seq", "tp"),
            P("tp", None),
            P(),
            P(),
            P("seq", ("group", "tp")),
            P(("group", "tp"), None),
            P("seq", None),
            P(("group", "seq")),
            P(),
            P(),
            P(),
        ),
        out_specs=(P(("group", "seq"), None), P(("group", "seq"), "tp")),
        check_vma=False,
    )
```

```python
import functools
import jax
import jax.numpy as jnp
from jax import lax
from jax.experimental import pallas as pl
from jax.experimental.pallas import tpu as pltpu
from jax.sharding import PartitionSpec as P

FTOK = 2048
HALVES = 2
MESH = pl.DeviceIdType.MESH
F32 = jnp.float32
BF16 = jnp.bfloat16
ROOT = 0.7978845608028654
CUBE = 0.044715


def split_bf16(v):
    hi = lax.reduce_precision(v, 8, 7)
    return hi.astype(BF16), (v - hi).astype(BF16)


def gelu_tanh(v):
    return 0.5 * v * (1.0 + jnp.tanh(ROOT * (v + CUBE * v * v * v)))


def dot(a, b):
    return jnp.dot(a, b, preferred_element_type=F32)


def dot_t(a, b):
    return lax.dot_general(a, b, (((1,), (1,)), ((), ())), preferred_element_type=F32)


def kernel(
    ng, ns, nt, shared, pieces,
    hidden_in, gain_in, weights, gen_head, embed_in, scaling, crit_value_in, crit_head, noise, owner, tsteps, tables, weighting,
    latent_out, grad_out,
    hidden, embed, crit_value, load_sem, gain, wall, normed, inv_ref, values, slope, mpart, mall, hall, noise_all, latp, gapp, inn,
    send_r, send_l, recv_r, recv_l, total,
    own_part, own_sem, w_send, w_recv, f_send, f_recv, m_send, m_recv, n_send, n_recv,
    g_send, g_recv, h_send, h_recv, t_send, t_recv, rs_sem, rr_sem, ls_sem, lr_sem,
):
    g = lax.axis_index("group")
    s = lax.axis_index("seq")
    t = lax.axis_index("tp")
    rows, width = hidden_in.shape
    depth = weights.shape[0]
    crit_rows = noise.shape[1]
    half = channels = noise.shape[0]
    columns = width // nt
    pending = []

    def seq_peer(o):
        return lax.rem(s + o, ns)

    def group_peer(o):
        return lax.rem(g + o, ng)

    def tp_peer(o):
        return lax.rem(t + o, nt)

    def push(src, dst, send, recv, where):
        copy = pltpu.make_async_remote_copy(
            src_ref=src, dst_ref=dst, send_sem=send, recv_sem=recv,
            device_id=where, device_id_type=MESH,
        )
        copy.start()
        pending.append(copy)
        return copy

    loads = []
    for k, (src, dst) in enumerate(((hidden_in, hidden), (crit_value_in, crit_value), (embed_in, embed))):
        loads.append(pltpu.make_async_copy(src, dst, load_sem.at[k]))
        loads[-1].start()

    barrier = pltpu.get_barrier_semaphore()
    for o in range(1, ns):
        pl.semaphore_signal(barrier, inc=1, device_id={"seq": seq_peer(o)}, device_id_type=MESH)
    for o in range(1, ng):
        pl.semaphore_signal(barrier, inc=1, device_id={"group": group_peer(o)}, device_id_type=MESH)
    for o in range(1, nt):
        pl.semaphore_signal(barrier, inc=1, device_id={"tp": tp_peer(o)}, device_id_type=MESH)
    pl.semaphore_wait(barrier, ns + ng + nt - 3)

    local = pltpu.make_async_copy(weights, wall.at[pl.ds(s * depth, depth), :], own_sem)
    local.start()
    quarter = depth // ng if shared else depth
    step = quarter // pieces
    mine = g * quarter if shared else 0
    w_copies = {}
    for p in range(pieces):
        for o in range(1, ns):
            w_copies[o, p] = push(
                weights.at[pl.ds(mine + p * step, step), :],
                wall.at[pl.ds(s * depth + mine + p * step, step), :],
                w_send.at[o - 1, p], w_recv.at[o - 1, p], {"seq": seq_peer(o)},
            )
    h_copies = [
        push(crit_head, hall.at[g], h_send.at[o - 1], h_recv.at[o - 1], {"group": group_peer(o)})
        for o in range(1, ng)
    ]
    noise_all[s] = noise[...]
    hall[g] = crit_head[...]

    def fold():
        if depth % 128 == 0:
            critic = g // (ng // 2)
            at = pl.ds(pl.multiple_of(s * depth, 128), depth)
            both = scaling[:, at].astype(F32)
            eg = embed[critic, :, at].astype(F32) * jnp.where(critic == 0, both[0:1], both[1:2])
            eg_high = eg.astype(BF16)
            eg_low = (eg - eg_high.astype(F32)).astype(BF16)
            eg_pair = jnp.concatenate([eg_high, eg_low], axis=0)
        else:
            eg_pair = scaling[...]
        folded = dot_t(eg_pair, crit_value[...])
        mpart[s] = folded[:half] + folded[half:]

    def norm_all():
        gain[...] = gain_in[...].astype(F32).reshape(1, width)

        def norm_rows(r, carry):
            at = pl.ds(pl.multiple_of(r * 32, 32), 32)
            x = hidden[at, :].astype(F32)
            inverse = lax.rsqrt(jnp.mean(x * x, axis=-1, keepdims=True) + 1e-06)
            normed[at, :] = (x * inverse * gain[...]).astype(BF16)
            inv_ref[at, :] = jnp.broadcast_to(inverse, (32, 128))
            return carry

        lax.fori_loop(0, rows // 32, norm_rows, 0)
        values[...] = jnp.zeros_like(values)

    def add_rows(start, size):
        at = pl.multiple_of(start, 128)
        values[...] += dot(normed[:, pl.ds(at, size)], wall[pl.ds(at, size), :])

    def own_rows(j, carry):
        add_rows(s * depth + j * quarter, quarter)
        return carry

    x_copies, c_copies, d_copies = {}, {}, {}

    def forward(p):
        for o in range(1, ns):
            w_copies[o, p].wait_recv()
            base = lax.rem(s - o + ns, ns) * depth
            at = pl.ds(base + mine + p * step, step)
            x_copies[o, p] = push(
                wall.at[at, :], wall.at[at, :],
                f_send.at[0, o - 1, p], f_recv.at[0, o - 1, p], {"group": g ^ 2},
            )
            c_copies[o, p] = push(
                wall.at[at, :], wall.at[at, :],
                f_send.at[1, o - 1, p], f_recv.at[1, o - 1, p], {"group": g ^ 1},
            )

    if shared:
        forward(0)
    loads[0].wait()
    norm_all()
    if shared:
        forward(1)
        forward(2)
    local.wait()
    if shared:
        lax.fori_loop(0, ng, own_rows, 0)
        forward(3)
    loads[1].wait()
    loads[2].wait()
    fold()
    if shared:
        for p in range(4, pieces):
            forward(p)
    n_copies = [
        push(noise, noise_all.at[s], n_send.at[o - 1], n_recv.at[o - 1], {"seq": seq_peer(o)})
        for o in range(1, ns)
    ]
    m_copies = [
        push(mpart.at[s], mpart.at[s], m_send.at[o - 1], m_recv.at[o - 1], {"seq": seq_peer(o)})
        for o in range(1, ns)
    ]
    if shared:
        for p in range(pieces):
            for o in range(1, ns):
                x_copies[o, p].wait_recv()
                base = lax.rem(s - o + ns, ns) * depth
                at = pl.ds(base + (g ^ 2) * quarter + p * step, step)
                d_copies[o, p] = push(
                    wall.at[at, :], wall.at[at, :],
                    f_send.at[2, o - 1, p], f_recv.at[2, o - 1, p], {"group": g ^ 1},
                )

    for copy in m_copies:
        copy.wait_recv()
    whole = mpart[0]
    for k in range(1, ns):
        whole = whole + mpart[k]
    high = whole.astype(BF16)
    high32 = high.astype(F32)
    cols = whole.shape[1]
    fill = -cols % 128
    both = jnp.concatenate([high32, whole - high32], axis=0)
    if fill:
        both = jnp.concatenate([both, jnp.zeros((2 * half, fill), F32)], axis=1)
    mall[g] = both.T[:cols].astype(BF16)
    g_copies = [
        push(mall.at[g], mall.at[g], g_send.at[o - 1], g_recv.at[o - 1], {"group": group_peer(o)})
        for o in range(1, ng)
    ]
    grams = []
    for which in range(2):
        gram = dot_t(embed[which], embed[which])
        first = gram.astype(BF16)
        rest = gram - first.astype(F32)
        second = rest.astype(BF16)
        grams.append((first, second, (rest - second.astype(F32)).astype(BF16)))
    for copy in n_copies:
        copy.wait_recv()

    def pick(k, carry):
        place = lax.broadcasted_iota(jnp.int32, (crit_rows, rows), 0) + k * crit_rows
        hot = jnp.where(place == owner_row, 1.0, 0.0).astype(BF16)
        return carry + dot(noise_all[k], hot)

    owner_row = owner[...].reshape(1, rows)
    noise_rows = lax.fori_loop(0, ns, pick, jnp.zeros((channels, rows), F32))
    level = tsteps[((g * ns + s) * rows) // FTOK]
    levels = tables.shape[1]
    found = lax.broadcasted_iota(jnp.int32, (1, levels), 1) == level
    mix = jnp.sum(jnp.where(found, tables[...], 0.0), axis=1, keepdims=True)
    weight = jnp.sum(jnp.where(found, weighting[...].reshape(1, levels), 0.0), axis=1, keepdims=True)

    if shared:
        for o in range(1, ns):
            base = lax.rem(s - o + ns, ns) * depth
            add_rows(base + g * quarter, quarter)
            add_rows(base + (g ^ 2) * quarter, quarter)
            for p in range(pieces):
                c_copies[o, p].wait_recv()
            add_rows(base + (g ^ 1) * quarter, quarter)
            for p in range(pieces):
                d_copies[o, p].wait_recv()
            add_rows(base + (g ^ 3) * quarter, quarter)
    else:
        for copy in w_copies.values():
            copy.wait_recv()

        def all_rows(j, carry):
            add_rows(j * (width // 8), width // 8)
            return carry

        lax.fori_loop(0, 8, all_rows, 0)

    def share_tp(buffer, index):
        return [
            push(buffer.at[t], buffer.at[t], t_send.at[index, o - 1], t_recv.at[index, o - 1], {"tp": tp_peer(o)})
            for o in range(1, nt)
        ]

    def sum_tp(buffer, copies):
        for copy in copies:
            copy.wait_recv()
        out = buffer[0].astype(F32)
        for k in range(1, nt):
            out = out + buffer[k].astype(F32)
        return out

    v = values[...]
    tanh = jnp.tanh(ROOT * (v + CUBE * v * v * v))
    latp[t] = dot_t(gen_head[...], (0.5 * v * (1.0 + tanh)).astype(BF16)).astype(BF16)
    lat_copies = share_tp(latp, 0)
    slope[...] = 0.5 * (1.0 + tanh) + 0.5 * v * (1.0 - tanh * tanh) * ROOT * (1.0 + 3.0 * CUBE * v * v)
    for copy in g_copies + h_copies:
        copy.wait_recv()
    latent = sum_tp(latp, lat_copies).astype(BF16)
    latent_out[...] = latent

    noisy = (mix[0:1] * latent.astype(F32) + mix[1:2] * noise_rows).astype(BF16)
    noisy32 = noisy.astype(F32)
    scales = []
    for which in range(2):
        a, b, c = grams[which]
        quad = jnp.sum((dot(a, noisy) + dot(b, noisy) + dot(c, noisy)) * noisy32, axis=0, keepdims=True)
        scales.append(lax.rsqrt(jnp.maximum(quad, 0.0) / width + 1e-06))
    pair = jnp.concatenate([noisy, noisy], axis=0)
    gap = jnp.zeros((channels, rows), F32)
    for member in range(ng):
        which = member // (ng // 2)
        act = gelu_tanh(dot(mall[member], pair) * scales[which]).astype(BF16)
        term = dot(hall[member], act)
        gap = gap + term if which else gap - term
    gapp[t] = gap.astype(BF16)
    gap = sum_tp(gapp, share_tp(gapp, 1))
    pull = weight * gap
    fill = -channels % 128
    if fill:
        pull = jnp.concatenate([pull, jnp.zeros((fill, rows), F32)], axis=0)
    cotangent = pull.T[:, :channels].astype(BF16)

    grad_values = (slope[...] * dot(cotangent, gen_head[...])).astype(BF16)
    inner = jnp.sum(grad_values.astype(F32) * values[...], axis=-1, keepdims=True)
    inn[t] = jnp.broadcast_to(inner, (rows, 128)).T[:8]
    inn_copies = share_tp(inn, 2)

    block = 256 if columns % 256 == 0 else columns
    part_rows = rows // HALVES

    def part(q, h, out):
        lhs = grad_values[h * part_rows:(h + 1) * part_rows]

        def one(j, carry):
            at = pl.ds(pl.multiple_of(j * block, block), block)
            w = wall[pl.ds(pl.multiple_of(q * columns + j * block, block), block), :]
            term = dot_t(lhs, w)
            out[:, at] = term.astype(out.dtype)
            return carry

        lax.fori_loop(0, columns // block, one, 0)

    def linker(to_right):
        buf_s, buf_r = (send_r, recv_r) if to_right else (send_l, recv_l)
        sem_s, sem_r = (rs_sem, rr_sem) if to_right else (ls_sem, lr_sem)

        def link(k, h):
            return pltpu.make_async_remote_copy(
                src_ref=buf_s.at[k, h], dst_ref=buf_r.at[k, h], send_sem=sem_s.at[k, h], recv_sem=sem_r.at[k, h],
                device_id={"tp": t + 1 if to_right else t - 1}, device_id_type=MESH,
            )

        return buf_s, buf_r, link

    def chain(d, h, to_right):
        buf_s, buf_r, link = linker(to_right)
        target = t + d if to_right else t - d
        inside = target <= nt - 1 if to_right else target >= 0
        starts = t == 0 if to_right else t == nt - 1
        further = target + 1 <= nt - 1 if to_right else target - 1 >= 0

        @pl.when(inside)
        def _():
            if d < nt - 1:
                @pl.when(starts)
                def _():
                    part(target, h, buf_s.at[d - 1, h])
                    link(d, h).wait_send()

                @pl.when(jnp.logical_not(starts))
                def _():
                    part(target, h, own_part)
                    link(d, h).wait_recv()
                    buf_s[d - 1, h] = (own_part[...] + buf_r[d, h].astype(F32)).astype(BF16)
                    if d < nt - 2:
                        @pl.when(further)
                        def _():
                            link(d, h).wait_send()
            else:
                part(target, h, buf_s.at[d - 1, h])
            link(d - 1, h).start()

    def chain_end(h, to_right):
        buf_s, buf_r, link = linker(to_right)
        at = pl.ds(h * part_rows, part_rows)

        @pl.when(t > 0 if to_right else t < nt - 1)
        def _():
            link(0, h).wait_recv()
            total[at, :] += buf_r[0, h].astype(F32)

        @pl.when(t < nt - 1 if to_right else t > 0)
        def _():
            link(0, h).wait_send()

    for d in range(nt - 1, 0, -1):
        for h in range(HALVES):
            chain(d, h, True)
            chain(d, h, False)
    for h in range(HALVES):
        part(t, h, total.at[pl.ds(h * part_rows, part_rows), :])
    inner_all = sum_tp(inn, inn_copies)
    inner_col = jnp.broadcast_to(inner_all[0:1], (128, rows)).T[:, :1]
    for h in range(HALVES):
        chain_end(h, True)
        chain_end(h, False)
    inverse = inv_ref[:, :1]
    mixed = inner_col / (inverse * width)
    factor = inverse * inverse * inverse * mixed

    def finish(j, carry):
        at = pl.ds(pl.multiple_of(j * block, block), block)
        far = pl.ds(pl.multiple_of(t * columns + j * block, block), block)
        scaled = total[:, at] * gain[:, far]
        grad_out[:, at] = (inverse * scaled - hidden[:, far].astype(F32) * factor).astype(BF16)
        return carry

    lax.fori_loop(0, columns // block, finish, 0)
    for copy in pending:
        copy.wait_send()


def local(
    hidden,
    norm_gain,
    gen_value,
    gen_head,
    critic_embed,
    critic_gain,
    critic_value,
    critic_head,
    noise,
    owner,
    tsteps,
    noise_mix,
    gap_weight,
):
    rows, width = hidden.shape
    depth, heads = gen_value.shape
    crit_rows, latent_width = noise.shape
    crit_cols = critic_value.shape[1]
    ns = lax.axis_size("seq")
    ng = lax.axis_size("group")
    nt = lax.axis_size("tp")
    group_id = lax.axis_index("group")
    seq_id = lax.axis_index("seq")
    if depth % 128 == 0:
        scaling = critic_gain
    else:
        critic_id = group_id // (ng // 2)
        first = seq_id * depth
        embed = lax.dynamic_slice(critic_embed, (critic_id, 0, first), (1, latent_width, depth))[0]
        gains = lax.dynamic_slice(critic_gain, (critic_id, first), (1, depth))
        scaling = jnp.concatenate(split_bf16(embed.astype(F32) * gains.astype(F32)), axis=0)

    shared = ng == 4 and depth % (128 * ng) == 0
    pieces = 8 if shared else 1
    vmem = pl.BlockSpec(memory_space=pltpu.VMEM)
    far = pl.BlockSpec(memory_space=pl.ANY)
    columns = width // nt
    dma = pltpu.SemaphoreType.DMA
    latent, grad = pl.pallas_call(
        functools.partial(kernel, ng, ns, nt, shared, pieces),
        out_shape=(
            jax.ShapeDtypeStruct((latent_width, rows), BF16),
            jax.ShapeDtypeStruct((rows, columns), BF16),
        ),
        in_specs=[far, vmem, far, vmem, far, vmem, far] + [vmem] * 3
        + [pl.BlockSpec(memory_space=pltpu.SMEM), vmem, vmem],
        out_specs=(vmem, vmem),
        scratch_shapes=[
            pltpu.VMEM((rows, width), BF16),
            pltpu.VMEM(critic_embed.shape, BF16),
            pltpu.VMEM((crit_cols, depth), BF16),
            dma((3,)),
            pltpu.VMEM((1, width), F32),
            pltpu.VMEM((width, heads), BF16),
            pltpu.VMEM((rows, width), BF16),
            pltpu.VMEM((rows, 128), F32),
            pltpu.VMEM((rows, heads), F32),
            pltpu.VMEM((rows, heads), F32),
            pltpu.VMEM((ns, latent_width, crit_cols), F32),
            pltpu.VMEM((ng, crit_cols, 2 * latent_width), BF16),
            pltpu.VMEM((ng, latent_width, crit_cols), BF16),
            pltpu.VMEM((ns, latent_width, crit_rows), BF16),
            pltpu.VMEM((nt, latent_width, rows), BF16),
            pltpu.VMEM((nt, latent_width, rows), BF16),
            pltpu.VMEM((nt, 8, rows), F32),
            pltpu.VMEM((nt - 1, HALVES, rows // HALVES, columns), BF16),
            pltpu.VMEM((nt - 1, HALVES, rows // HALVES, columns), BF16),
            pltpu.VMEM((nt - 1, HALVES, rows // HALVES, columns), BF16),
            pltpu.VMEM((nt - 1, HALVES, rows // HALVES, columns), BF16),
            pltpu.VMEM((rows, columns), F32),
            pltpu.VMEM((rows // HALVES, columns), F32),
            dma,
            dma((ns - 1, pieces)),
            dma((ns - 1, pieces)),
            dma((3, ns - 1, pieces)),
            dma((3, ns - 1, pieces)),
            dma((ns - 1,)),
            dma((ns - 1,)),
            dma((ns - 1,)),
            dma((ns - 1,)),
            dma((ng - 1,)),
            dma((ng - 1,)),
            dma((ng - 1,)),
            dma((ng - 1,)),
            dma((3, nt - 1)),
            dma((3, nt - 1)),
            dma((nt - 1, HALVES)),
            dma((nt - 1, HALVES)),
            dma((nt - 1, HALVES)),
            dma((nt - 1, HALVES)),
        ],
        compiler_params=pltpu.CompilerParams(
            collective_id=0, has_side_effects=True, vmem_limit_bytes=56 * 1024 * 1024
        ),
    )(
        hidden, norm_gain, gen_value, gen_head.T, critic_embed, scaling, critic_value.T, critic_head.T,
        noise.T, owner, tsteps, noise_mix, gap_weight,
    )
    return latent.T, grad


def solution(mesh):
    return jax.shard_map(
        local,
        mesh=mesh,
        in_specs=(
            P(("group", "seq"), None),
            P(),
            P("seq", "tp"),
            P("tp", None),
            P(),
            P(),
            P("seq", ("group", "tp")),
            P(("group", "tp"), None),
            P("seq", None),
            P(("group", "seq")),
            P(),
            P(),
            P(),
        ),
        out_specs=(P(("group", "seq"), None), P(("group", "seq"), "tp")),
        check_vma=False,
    )
```
